128 devices in a mesh: fsdp: 16 (over z_hi, y, core), ctx: 2 (over z_lo), tp: 4 (over x).
Axes of the slice: x: 4, y: 4, z: 4 (z_hi: 2, z_lo: 2; z = z_hi * 2 + z_lo), core: 2. Of those that a mesh axis runs over, the one named last changes fastest.
Arguments:
- tokens: bfloat16 [16, 1536, 1024], P('fsdp', 'ctx'), may hold values from -6 to 6
- norm_gain: bfloat16 [1024], replicated, may hold values from 0.5 to 1.5
- in_weight: bfloat16 [1024, 3, 1024], P('fsdp', None, 'tp'), may hold values from -0.1875 to 0.1875
- conv_weight: bfloat16 [3, 1024], P(None, 'tp'), may hold values from -3 to 3
- out_weight: bfloat16 [1024, 1024], P('tp', 'fsdp'), may hold values from -0.1875 to 0.1875
- ffn_gain: bfloat16 [1024], replicated, may hold values from 0.5 to 1.5
- gate_up_weight: bfloat16 [2, 1024, 4608], P(None, 'fsdp', 'tp'), may hold values from -0.1875 to 0.1875
- down_weight: bfloat16 [4608, 1024], P('tp', 'fsdp'), may hold values from -0.125 to 0.125
- cotangent: bfloat16 [16, 1536, 1024], P('fsdp', 'ctx'), may hold values from -6 to 6
Outputs:
- output: bfloat16 [16, 1536, 1024], P('fsdp', 'ctx')
- input_grad: bfloat16 [16, 1536, 1024], P('fsdp', 'ctx')
- norm_gain_grad: float32 [1024], replicated
- in_weight_grad: float32 [1024, 3, 1024], P('fsdp', None, 'tp')
- conv_weight_grad: float32 [3, 1024], P(None, 'tp')
- out_weight_grad: float32 [1024, 1024], P('tp', 'fsdp')
- ffn_gain_grad: float32 [1024], replicated
- gate_up_grad: float32 [2, 1024, 4608], P(None, 'fsdp', 'tp')
- down_weight_grad: float32 [4608, 1024], P('tp', 'fsdp')
The draws below stay inside these ranges and needn't reach their ends.
All inputs are finite; a program needn't handle non-finite values.
Results may differ from the reference program's by a relative error of at most 0.018.
Values may be sent and summed in bfloat16 or wider, within the bound.
No kernel may reach another device: no remote copies, remote signals or barrier semaphores. Data moves between devices by JAX's collectives and lax.ppermute only.
A program may use at most 128 MiB of HBM per device.

```python
import jax
import jax.numpy as jnp
from jax import lax

D = 1024
FF = 4608
KERNEL = 3
LEN = 1536
SEQS = 16


def shard_levels(own_key, shape, split, least, largest):
    factor_of, own = 1.0, jax.random.fold_in(own_key, 6)
    for dim, parts in split:
        draws = jnp.exp(jax.random.uniform(jax.random.fold_in(own, dim), (parts,), jnp.float32, least / len(split), largest / len(split)))
        factor_of = factor_of * jnp.repeat(draws, shape[dim] // parts).reshape([-1 if axis == dim else 1 for axis in range(len(shape))])
    return factor_of


def bell_draw(rng, dims, scale, reach, pieces=(), kind=jnp.bfloat16):
    entries = scale * jax.random.normal(rng, dims, jnp.float32)
    if pieces:
        entries = entries * shard_levels(rng, dims, pieces, -0.22, 0.18)
    return jnp.clip(entries, -reach, reach).astype(kind)


def setup_inputs(seed: int = 0) -> dict:
    key_list = jax.random.split(jax.random.key(seed), 10)
    return {
        "tokens": bell_draw(key_list[0], (SEQS, LEN, D), 1.0, 6.0, ((0, 16), (1, 2))),
        "norm_gain": jnp.clip(1.0 + 0.1 * jax.random.normal(key_list[1], (D,), jnp.float32), 0.5, 1.5).astype(jnp.bfloat16),
        "in_weight": bell_draw(key_list[2], (D, 3, D), D ** -0.5, 0.1875, ((0, 16), (2, 4))),
        "conv_weight": bell_draw(key_list[3], (KERNEL, D), 0.6, 3.0, ((1, 4),)),
        "out_weight": bell_draw(key_list[4], (D, D), D ** -0.5, 0.1875, ((0, 4), (1, 16))),
        "ffn_gain": jnp.clip(1.0 + 0.1 * jax.random.normal(key_list[5], (D,), jnp.float32), 0.5, 1.5).astype(jnp.bfloat16),
        "gate_up_weight": bell_draw(key_list[6], (2, D, FF), D ** -0.5, 0.1875, ((1, 16), (2, 4))),
        "down_weight": bell_draw(key_list[7], (FF, D), (FF // 2) ** -0.5, 0.125, ((0, 4), (1, 16))),
        "cotangent": bell_draw(key_list[8], (SEQS, LEN, D), 1.0, 6.0, ((0, 16), (1, 2))),
    }


@jax.custom_vjp
def low(v):
    return lax.optimization_barrier(v.astype(jnp.bfloat16)).astype(jnp.float32)

@jax.custom_vjp
def low_back(v):
    return v

def low_keep(v):
    return (low(v), None)

def low_pass(kept, grad):
    return (grad,)

def back_keep(v):
    return (v, None)

def back_low(kept, grad):
    return (low(grad),)
low.defvjp(low_keep, low_pass)
low_back.defvjp(back_keep, back_low)
EPSILON = 1e-05
HIGH = lax.Precision.HIGHEST

def rms_scaled(values, gain_vec):
    inv_rms = lax.rsqrt(lax.optimization_barrier(jnp.mean(values * values, axis=-1, keepdims=True)) + EPSILON)
    return values * inv_rms * gain_vec

def mixer_block(sequence, norm_gain, in_weight, conv_taps, out_weight, ffn_gain, gate_up_weight, down_weight):
    normed_in = low(rms_scaled(sequence, norm_gain))
    projected = low_back(jnp.einsum('td,dkc->tkc', normed_in, in_weight, precision=HIGH))
    gate_b = projected[:, 0]
    gate_c = projected[:, 1]
    values_v = projected[:, 2]
    mixed_in = low_back(low(gate_b * values_v))
    padded = jnp.concatenate([jnp.zeros((2, mixed_in.shape[1]), jnp.float32), mixed_in], 0)
    conv_out = conv_taps[0] * padded[:-2] + conv_taps[1] * padded[1:-1] + conv_taps[2] * padded[2:]
    gated = low(gate_c * conv_out)
    mixer_out = low_back(jnp.dot(gated, out_weight, precision=HIGH))
    middle = sequence + mixer_out
    normed_mid = low(rms_scaled(middle, ffn_gain))
    gate_up = jnp.einsum('td,kdf->tkf', normed_mid, gate_up_weight, precision=HIGH)
    gate_g = low_back(gate_up[:, 0])
    up_u = low_back(gate_up[:, 1])
    activated = low(jax.nn.silu(gate_g) * up_u)
    ffn_out = low_back(jnp.dot(activated, down_weight, precision=HIGH))
    return middle + ffn_out

def reference(tokens, norm_gain, in_weight, conv_weight, out_weight, ffn_gain, gate_up_weight, down_weight, cotangent):
    weights = tuple((w.astype(jnp.float32) for w in (norm_gain, in_weight, conv_weight, out_weight, ffn_gain, gate_up_weight, down_weight)))

    def one_sequence(carry, inputs_pair):
        sequence, seq_grad = inputs_pair
        result, pullback = jax.vjp(mixer_block, sequence.astype(jnp.float32), *weights)
        grads = pullback(seq_grad.astype(jnp.float32))
        carry = tuple((total + piece for total, piece in zip(carry, grads[1:])))
        return (carry, (result.astype(jnp.bfloat16), grads[0].astype(jnp.bfloat16)))
    zeros_init = tuple((jnp.zeros(w.shape, jnp.float32) for w in weights))
    totals, (outputs, input_grads) = lax.scan(one_sequence, zeros_init, (tokens, cotangent))
    return (outputs, input_grads, totals[0], totals[1], totals[2], totals[3], totals[4], totals[5], totals[6])
```

```python
import jax
import jax.numpy as jnp
from jax import lax
from jax.sharding import PartitionSpec as P

EPSILON = 1e-05
BF = jnp.bfloat16
F32 = jnp.float32
NX, NY = 4, 4
ROWS = 192


def x_shift(v, d):
    return lax.ppermute(v, "tp", [(i, (i + d) % NX) for i in range(NX)])


def y_shift(v, d):
    route = []
    for f in range(16):
        zh, y, c = f // 8, (f // 2) % 4, f % 2
        route.append((f, zh * 8 + ((y + d) % NY) * 2 + c))
    return lax.ppermute(v, "fsdp", route)


def core_swap(v):
    return lax.ppermute(v, "fsdp", [(f, f ^ 1) for f in range(16)])


def z_cross(v):
    route = []
    for f in range(16):
        for c in range(2):
            route.append((f * 2 + c, (f ^ 8) * 2 + (c ^ 1)))
    return lax.ppermute(v, ("fsdp", "ctx"), route)


def ctx_swap(v):
    return lax.ppermute(v, "ctx", [(0, 1), (1, 0)])


def passed_along(block, distance):
    route = [(0, 1)] if distance == 1 else [(1, 0)]
    return lax.ppermute(block, "ctx", route)


def dot(a, b, dims=(((1,), (0,)), ((), ()))):
    return lax.dot_general(a, b, dims, preferred_element_type=F32)


CC = (((1,), (1,)), ((), ()))
RR = (((0,), (0,)), ((), ()))


def inv_rms_of(v):
    return lax.rsqrt(jnp.mean(v * v, axis=-1, keepdims=True) + EPSILON)


def place(pieces, spots, axis=0):
    size = pieces[0].shape[axis]
    shape = list(pieces[0].shape)
    shape[axis] = size * len(pieces)
    out = jnp.zeros(shape, pieces[0].dtype)
    for piece, spot in zip(pieces, spots):
        out = lax.dynamic_update_slice_in_dim(out, piece, spot * size, axis)
    return out


def block(v, spot, size=ROWS, axis=0):
    return lax.dynamic_slice_in_dim(v, spot * size, size, axis)


def gather_x(v):
    return [v, x_shift(v, 1), x_shift(v, -1), x_shift(v, 2)]


def scatter_x(parts):
    got = [
        x_shift(parts[3].astype(BF), 2),
        x_shift(parts[1].astype(BF), -1),
        x_shift(parts[2].astype(BF), 1),
    ]
    return parts[0] + got[0].astype(F32) + got[1].astype(F32) + got[2].astype(F32)


def body(
    tokens,
    norm_gain,
    in_weight,
    conv_weight,
    out_weight,
    ffn_gain,
    gate_up_weight,
    down_weight,
    cotangent,
):
    in_shape = tokens.shape
    width = in_shape[-1]
    tok = tokens.reshape(-1, width)
    cot = cotangent.reshape(-1, width)
    rows = tok.shape[0]
    fi = lax.axis_index("fsdp")
    zh, y, core = fi // 8, (fi // 2) % 4, fi % 2
    x = lax.axis_index("tp")
    spots = [x, (x + 3) % 4, (x + 1) % 4, (x + 2) % 4]
    gain1 = norm_gain.astype(F32)
    gain2 = ffn_gain.astype(F32)
    taps = conv_weight.astype(F32)

    packed_ffn = jnp.concatenate([gate_up_weight, down_weight.T[None]], 0)
    w_ffn = lax.all_gather(packed_ffn, "fsdp", axis=1, tiled=True)

    mine = jnp.concatenate([in_weight.reshape(64, 768), out_weight.T], 1)
    other = z_cross(mine)
    pair = place([mine[None], other[None]], [zh, 1 - zh])
    ys = [pair, y_shift(pair, 1), y_shift(pair, -1), y_shift(pair, 2)]
    col = place([v[:, None] for v in ys], [y, (y + 3) % 4, (y + 1) % 4, (y + 2) % 4], 1)
    col2 = core_swap(col)
    w_mix = place([col[:, :, None], col2[:, :, None]], [core, 1 - core], 2).reshape(width, 1024)
    w_in = w_mix[:, :768]
    w_out_t = w_mix[:, 768:]

    x32 = tok.astype(F32)
    inv1 = inv_rms_of(x32)
    normed1 = x32 * inv1
    normed_in = (normed1 * gain1).astype(BF)
    projected = dot(normed_in, w_in)
    gate_b, gate_c, values_v = projected[:, :256], projected[:, 256:512], projected[:, 512:]
    mixed_in = (gate_b * values_v).astype(BF)
    arrived = passed_along(mixed_in[rows - 2 :], 1)
    extended = jnp.concatenate([arrived, mixed_in], 0).astype(F32)
    conv_out = (
        taps[0] * extended[:rows] + taps[1] * extended[1 : rows + 1] + taps[2] * extended[2:]
    )
    gated = (gate_c * conv_out).astype(BF)
    mixer_part = dot(gated, w_out_t, CC)
    own_tok = block(tok, x).astype(F32)
    middle = own_tok + scatter_x([block(mixer_part, s) for s in spots])

    inv2 = inv_rms_of(middle)
    normed2 = middle * inv2
    nm = gather_x((normed2 * gain2).astype(BF))
    cots = [block(cot, s) for s in spots]
    w_g, w_u, w_dt = w_ffn[0], w_ffn[1], w_ffn[2]
    acts, ggs, gus, ffns, mids = [], [], [], [], []
    for piece, ct in zip(nm, cots):
        gate_g = dot(piece, w_g)
        up_u = dot(piece, w_u)
        sg = jax.nn.sigmoid(gate_g)
        silu = gate_g * sg
        act = (silu * up_u).astype(BF)
        grad_act = dot(ct, w_dt)
        gg = (grad_act * up_u * sg * (1.0 + gate_g * (1.0 - sg))).astype(BF)
        gu = (grad_act * silu).astype(BF)
        ffns.append(dot(act, w_dt, CC))
        mids.append(dot(gg, w_g, CC) + dot(gu, w_u, CC))
        acts.append(act)
        ggs.append(gg)
        gus.append(gu)
    ffns[0] = ffns[0] + middle
    out_part = place([f.astype(BF) for f in ffns], spots)
    result = lax.psum(out_part, "tp").reshape(in_shape)
    grad_mid_in = scatter_x(mids)
    nm_all = jnp.concatenate(nm, 0)
    cot_all = jnp.concatenate(cots, 0)
    act_all = jnp.concatenate(acts, 0)
    gg_all = jnp.concatenate(ggs, 0)
    gu_all = jnp.concatenate(gus, 0)
    g_ffn = jnp.stack(
        [dot(nm_all, gg_all, RR), dot(nm_all, gu_all, RR), dot(cot_all, act_all, RR)], 0
    ).astype(BF)

    cot_own = cots[0].astype(F32)
    sv = grad_mid_in * gain2
    grad_middle = cot_own + inv2 * (sv - normed2 * jnp.mean(sv * normed2, -1, keepdims=True))
    gain2_part = jnp.sum(grad_mid_in * normed2, 0)
    grad_branch = place(gather_x(grad_middle.astype(BF)), spots)

    grad_gated = dot(grad_branch, w_out_t)
    g_out_t = dot(grad_branch, gated, RR)
    grad_c = grad_gated * conv_out
    grad_conv = grad_gated * gate_c
    taps_part = jnp.stack(
        [
            jnp.sum(extended[:rows] * grad_conv, 0),
            jnp.sum(extended[1 : rows + 1] * grad_conv, 0),
            jnp.sum(extended[2:] * grad_conv, 0),
        ],
        0,
    )
    back = passed_along(grad_conv[:2], -1)
    padded = jnp.concatenate([grad_conv, back], 0)
    grad_mixed = taps[2] * padded[:rows] + taps[1] * padded[1 : rows + 1] + taps[0] * padded[2:]
    rounded = grad_mixed.astype(BF).astype(F32)
    grad_proj = jnp.concatenate([rounded * values_v, grad_c, rounded * gate_b], 1).astype(BF)
    norm_part = dot(grad_proj, w_in, CC)
    gain1_part = jnp.sum(norm_part * normed1, 0)
    grad_norm_in = scatter_x([block(norm_part, s) for s in spots])
    g_in = dot(normed_in, grad_proj, RR)
    g_mix = jnp.concatenate([g_in, g_out_t], 1).astype(BF)

    inv1_own = inv_rms_of(own_tok)
    normed1_own = own_tok * inv1_own
    su = grad_norm_in * gain1
    grad_rows = grad_middle + inv1_own * (
        su - normed1_own * jnp.mean(su * normed1_own, -1, keepdims=True)
    )
    input_grad = place(gather_x(grad_rows.astype(BF)), spots).reshape(in_shape)

    def reduce_grads(g):
        n, _, m = g.shape
        g = g.reshape(n, 2, 4, 2, 64, m)
        send = lax.dynamic_index_in_dim(g, 1 - core, 3, False)
        keep = lax.dynamic_index_in_dim(g, core, 3, False)
        h = (keep.astype(F32) + core_swap(send).astype(F32)).astype(BF)
        part = [lax.dynamic_index_in_dim(h, s, 2, False) for s in (y, (y + 3) % 4, (y + 1) % 4, (y + 2) % 4)]
        k = (
            part[0].astype(F32)
            + y_shift(part[1], -1).astype(F32)
            + y_shift(part[2], 1).astype(F32)
            + y_shift(part[3], 2).astype(F32)
        ).astype(BF)
        own = lax.dynamic_index_in_dim(k, zh, 1, False).astype(F32)
        far = lax.dynamic_index_in_dim(k, 1 - zh, 1, False)
        half = (own + z_cross(far).astype(F32)).astype(BF)
        return half.astype(F32) + ctx_swap(half).astype(F32)

    r_ffn = reduce_grads(g_ffn)
    r_mix = reduce_grads(g_mix[None])[0]

    small = jnp.concatenate([gain1_part, gain2_part, taps_part.reshape(-1)], 0).reshape(22, 128)
    small = small + core_swap(small)
    small = small + y_shift(small, 1) + y_shift(small, -1) + y_shift(small, 2)
    small = small + z_cross(small)
    small = small + ctx_swap(small)
    gains = small[:16]
    gains = gains + x_shift(gains, 1) + x_shift(gains, -1) + x_shift(gains, 2)
    return (
        result,
        input_grad,
        gains[:8].reshape(-1),
        r_mix[:, :768].reshape(64, 3, 256),
        small[16:].reshape(3, 256),
        r_mix[:, 768:].T,
        gains[8:].reshape(-1),
        r_ffn[:2],
        r_ffn[2].T,
    )


def solution(mesh):
    placed = (
        P("fsdp", "ctx", None),
        P(),
        P("fsdp", None, "tp"),
        P(None, "tp"),
        P("tp", "fsdp"),
        P(),
        P(None, "fsdp", "tp"),
        P("tp", "fsdp"),
        P("fsdp", "ctx", None),
    )
    return jax.shard_map(
        body,
        mesh=mesh,
        in_specs=placed,
        out_specs=(
            P("fsdp", "ctx", None),
            P("fsdp", "ctx", None),
            P(),
            P("fsdp", None, "tp"),
            P(None, "tp"),
            P("tp", "fsdp"),
            P(),
            P(None, "fsdp", "tp"),
            P("tp", "fsdp"),
        ),
        check_vma=False,
    )
```

```python
import jax
import jax.numpy as jnp
from jax import lax
from jax.sharding import PartitionSpec as P

EPSILON = 1e-05
BF = jnp.bfloat16
F32 = jnp.float32
NX, NY = 4, 4
ROWS = 192


def x_shift(v, d):
    return lax.ppermute(v, "tp", [(i, (i + d) % NX) for i in range(NX)])


def y_shift(v, d):
    route = []
    for f in range(16):
        zh, y, c = f // 8, (f // 2) % 4, f % 2
        route.append((f, zh * 8 + ((y + d) % NY) * 2 + c))
    return lax.ppermute(v, "fsdp", route)


def core_swap(v):
    return lax.ppermute(v, "fsdp", [(f, f ^ 1) for f in range(16)])


def z_cross(v):
    route = []
    for f in range(16):
        for c in range(2):
            route.append((f * 2 + c, (f ^ 8) * 2 + (c ^ 1)))
    return lax.ppermute(v, ("fsdp", "ctx"), route)


def ctx_swap(v):
    return lax.ppermute(v, "ctx", [(0, 1), (1, 0)])


def passed_along(block, distance):
    route = [(0, 1)] if distance == 1 else [(1, 0)]
    return lax.ppermute(block, "ctx", route)


def dot(a, b, dims=(((1,), (0,)), ((), ()))):
    return lax.dot_general(a, b, dims, preferred_element_type=F32)


CC = (((1,), (1,)), ((), ()))
RR = (((0,), (0,)), ((), ()))


def inv_rms_of(v):
    return lax.rsqrt(jnp.mean(v * v, axis=-1, keepdims=True) + EPSILON)


def place(pieces, spots, axis=0):
    size = pieces[0].shape[axis]
    shape = list(pieces[0].shape)
    shape[axis] = size * len(pieces)
    out = jnp.zeros(shape, pieces[0].dtype)
    for piece, spot in zip(pieces, spots):
        out = lax.dynamic_update_slice_in_dim(out, piece, spot * size, axis)
    return out


def block(v, spot, size=ROWS, axis=0):
    return lax.dynamic_slice_in_dim(v, spot * size, size, axis)


def gather_x(v):
    return [v, x_shift(v, 1), x_shift(v, -1), x_shift(v, 2)]


def tie(v, *deps):
    return lax.optimization_barrier((v,) + deps)[0]


def split(v):
    high = v.astype(BF)
    return jnp.concatenate([high, (v - high.astype(F32)).astype(BF)], 0)


def joined(v):
    half = v.shape[0] // 2
    return v[:half].astype(F32) + v[half:].astype(F32)


def scatter_x(parts):
    got = [
        x_shift(parts[3].astype(BF), 2),
        x_shift(parts[1].astype(BF), -1),
        x_shift(parts[2].astype(BF), 1),
    ]
    return parts[0] + got[0].astype(F32) + got[1].astype(F32) + got[2].astype(F32)


def core_stage(g, core):
    g = g.transpose(3, 1, 2, 0, 4, 5)
    send = lax.dynamic_index_in_dim(g, 1 - core, 0, False)
    keep = lax.dynamic_index_in_dim(g, core, 0, False)
    return (keep.astype(F32) + core_swap(send).astype(F32)).astype(BF)


def y_stage(h, y):
    at = lambda d: lax.dynamic_index_in_dim(h, (y + d) % 4, 1, False)
    opp, up, down = at(2), at(1), at(3)
    from_down = y_shift(opp[0], 1)
    from_up = y_shift(opp[1], -1)
    up = jnp.concatenate([(up[0].astype(F32) + from_down.astype(F32)).astype(BF)[None], up[1:]], 0)
    down = jnp.concatenate(
        [down[:1], (down[1].astype(F32) + from_up.astype(F32)).astype(BF)[None]], 0
    )
    one = y_shift(up, 1)
    two = y_shift(down, -1)
    return (at(0).astype(F32) + one.astype(F32) + two.astype(F32)).astype(BF)


def body(
    tokens,
    norm_gain,
    in_weight,
    conv_weight,
    out_weight,
    ffn_gain,
    gate_up_weight,
    down_weight,
    cotangent,
):
    in_shape = tokens.shape
    width = in_shape[-1]
    tok = tokens.reshape(-1, width)
    cot = cotangent.reshape(-1, width)
    rows = tok.shape[0]
    fi = lax.axis_index("fsdp")
    zh, y, core = fi // 8, (fi // 2) % 4, fi % 2
    x = lax.axis_index("tp")
    spots = [x, (x + 3) % 4, (x + 1) % 4, (x + 2) % 4]
    gain1 = norm_gain.astype(F32)
    gain2 = ffn_gain.astype(F32)
    taps = conv_weight.astype(F32)

    packed_ffn = jnp.concatenate([gate_up_weight, down_weight.T[None]], 0)
    w_ffn = lax.all_gather(packed_ffn, "fsdp", axis=1, tiled=True)

    mine = jnp.concatenate([in_weight.reshape(64, 768), out_weight.T], 1)
    other = z_cross(mine)
    pair = place([mine[None], other[None]], [zh, 1 - zh])
    ys = [pair, y_shift(pair, 1), y_shift(pair, -1), y_shift(pair, 2)]
    col = place([v[:, None] for v in ys], [y, (y + 3) % 4, (y + 1) % 4, (y + 2) % 4], 1)
    col2 = core_swap(col)
    w_mix = place([col[:, :, None], col2[:, :, None]], [core, 1 - core], 2).reshape(width, 1024)
    w_in = w_mix[:, :768]
    w_out_t = w_mix[:, 768:]

    x32 = tok.astype(F32)
    inv1 = inv_rms_of(x32)
    normed1 = x32 * inv1
    normed_in = (normed1 * gain1).astype(BF)
    projected = dot(normed_in, w_in)
    gate_b, gate_c, values_v = projected[:, :256], projected[:, 256:512], projected[:, 512:]
    mixed_in = (gate_b * values_v).astype(BF)
    arrived = passed_along(mixed_in[rows - 2 :], 1)
    extended = jnp.concatenate([arrived, mixed_in], 0).astype(F32)
    conv_out = (
        taps[0] * extended[:rows] + taps[1] * extended[1 : rows + 1] + taps[2] * extended[2:]
    )
    gated = (gate_c * conv_out).astype(BF)
    mixer_part = dot(gated, w_out_t, CC)
    own_tok = block(tok, x).astype(F32)
    middle = own_tok + scatter_x([block(mixer_part, s) for s in spots])

    inv2 = inv_rms_of(middle)
    normed2 = middle * inv2
    nm = gather_x((normed2 * gain2).astype(BF))
    cots = [block(cot, s) for s in spots]
    w_g, w_u, w_dt = w_ffn[0], w_ffn[1], w_ffn[2]
    acts, ggs, gus, ffns, mids = [], [], [], [], []
    for piece, ct in zip(nm, cots):
        gate_g = dot(piece, w_g)
        up_u = dot(piece, w_u)
        sg = jax.nn.sigmoid(gate_g)
        silu = gate_g * sg
        act = (silu * up_u).astype(BF)
        grad_act = dot(ct, w_dt)
        gg = (grad_act * up_u * sg * (1.0 + gate_g * (1.0 - sg))).astype(BF)
        gu = (grad_act * silu).astype(BF)
        ffns.append(dot(act, w_dt, CC))
        mids.append(dot(gg, w_g, CC) + dot(gu, w_u, CC))
        acts.append(act)
        ggs.append(gg)
        gus.append(gu)
    ffns[0] = ffns[0] + middle
    out_part = place([f.astype(BF) for f in ffns], spots)
    result = lax.psum(out_part, "tp").reshape(in_shape)
    grad_mid_in = scatter_x(mids)
    nm_all = tie(jnp.concatenate(nm, 0), *mids)
    cot_all = tie(jnp.concatenate(cots, 0), *mids)
    act_all = jnp.concatenate(acts, 0)
    gg_all = jnp.concatenate(ggs, 0)
    gu_all = jnp.concatenate(gus, 0)
    g_ffn = jnp.stack(
        [dot(nm_all, gg_all, RR), dot(nm_all, gu_all, RR), dot(cot_all, act_all, RR)], 0
    ).astype(BF)
    h_ffn = core_stage(g_ffn.reshape(3, 2, 4, 2, 64, 1152), core)

    cot_own = cots[0].astype(F32)
    sv = grad_mid_in * gain2
    grad_middle = cot_own + inv2 * (sv - normed2 * jnp.mean(sv * normed2, -1, keepdims=True))
    gain2_part = jnp.sum(grad_mid_in * normed2, 0)
    grad_branch = tie(grad_middle.astype(BF), h_ffn)
    branches = gather_x(grad_branch)
    h_ffn = tie(h_ffn, grad_branch)
    k_ffn = y_stage(h_ffn, y)

    grad_gated = place([dot(p, w_out_t) for p in branches], spots)
    grad_c = grad_gated * conv_out
    grad_conv = grad_gated * gate_c
    back = passed_along(grad_conv[:2], -1)
    padded = jnp.concatenate([grad_conv, back], 0)
    grad_mixed = taps[2] * padded[:rows] + taps[1] * padded[1 : rows + 1] + taps[0] * padded[2:]
    rounded = grad_mixed.astype(BF).astype(F32)
    grad_proj = jnp.concatenate([rounded * values_v, grad_c, rounded * gate_b], 1).astype(BF)
    norm_parts = [dot(block(grad_proj, s), w_in, CC) for s in spots]
    grad_norm_in = scatter_x(norm_parts)

    grad_proj_late = tie(grad_proj, *norm_parts)
    branch_all = tie(jnp.concatenate(branches, 0), *norm_parts)
    grad_conv_late = tie(grad_conv, *norm_parts)
    g_out_t = dot(branch_all, jnp.concatenate([block(gated, s) for s in spots], 0), RR)
    g_in = dot(normed_in, grad_proj_late, RR)
    g_mix = jnp.concatenate([g_in, g_out_t], 1).astype(BF)
    taps_part = jnp.stack(
        [
            jnp.sum(extended[:rows] * grad_conv_late, 0),
            jnp.sum(extended[1 : rows + 1] * grad_conv_late, 0),
            jnp.sum(extended[2:] * grad_conv_late, 0),
        ],
        0,
    )
    gain1_part = sum(
        jnp.sum(p * block(normed1, s), 0) for p, s in zip(norm_parts, spots)
    )
    small = jnp.concatenate(
        [gain1_part, gain2_part, taps_part.reshape(-1), jnp.zeros((256,), F32)], 0
    ).reshape(3, 1024)
    small = jnp.concatenate([small, jnp.zeros((5, 1024), F32)], 0)

    g_mix = g_mix.reshape(2, 4, 2, 64, 1024)
    send = lax.dynamic_index_in_dim(g_mix, 1 - core, 2, False).reshape(512, 1024)
    keep = lax.dynamic_index_in_dim(g_mix, core, 2, False).reshape(512, 1024)
    got = core_swap(jnp.concatenate([send, split(small)], 0))
    h = (keep.astype(F32) + got[:512].astype(F32)).astype(BF).reshape(2, 4, 64, 1024)
    small = small + joined(got[512:])
    small_y = split(small)

    def y_piece(d):
        piece = lax.dynamic_index_in_dim(h, (y + d) % 4, 1, False).reshape(128, 1024)
        return y_shift(jnp.concatenate([piece, small_y], 0), d)

    k = lax.dynamic_index_in_dim(h, y, 1, False).reshape(128, 1024).astype(F32)
    for got in (y_piece(2), y_piece(1), y_piece(3)):
        k = k + got[:128].astype(F32)
        small = small + joined(got[128:])
    k = k.astype(BF).reshape(2, 64, 1024)
    far = lax.dynamic_index_in_dim(k, 1 - zh, 0, False)
    got = z_cross(jnp.concatenate([far, split(small)], 0))
    half = (lax.dynamic_index_in_dim(k, zh, 0, False).astype(F32) + got[:64].astype(F32)).astype(BF)
    small = small + joined(got[64:])
    got = ctx_swap(jnp.concatenate([half, split(small)], 0))
    r_mix = half.astype(F32) + got[:64].astype(F32)
    small = small + joined(got[64:])
    gains = small[:2].reshape(16, 128)
    gains = gains + x_shift(gains, 1) + x_shift(gains, -1) + x_shift(gains, 2)

    own = lax.dynamic_index_in_dim(k_ffn, zh, 0, False).astype(F32)
    far = lax.dynamic_index_in_dim(k_ffn, 1 - zh, 0, False)
    half = (own + z_cross(far).astype(F32)).astype(BF)
    r_ffn = half.astype(F32) + ctx_swap(half).astype(F32)

    inv1_own = inv_rms_of(own_tok)
    normed1_own = own_tok * inv1_own
    su = grad_norm_in * gain1
    grad_rows = grad_middle + inv1_own * (
        su - normed1_own * jnp.mean(su * normed1_own, -1, keepdims=True)
    )
    input_grad = place(gather_x(grad_rows.astype(BF)), spots).reshape(in_shape)

    return (
        result,
        input_grad,
        gains[:8].reshape(-1),
        r_mix[:, :768].reshape(64, 3, 256),
        small[2, :768].reshape(3, 256),
        r_mix[:, 768:].T,
        gains[8:].reshape(-1),
        r_ffn[:2],
        r_ffn[2].T,
    )


def solution(mesh):
    placed = (
        P("fsdp", "ctx", None),
        P(),
        P("fsdp", None, "tp"),
        P(None, "tp"),
        P("tp", "fsdp"),
        P(),
        P(None, "fsdp", "tp"),
        P("tp", "fsdp"),
        P("fsdp", "ctx", None),
    )
    return jax.shard_map(
        body,
        mesh=mesh,
        in_specs=placed,
        out_specs=(
            P("fsdp", "ctx", None),
            P("fsdp", "ctx", None),
            P(),
            P("fsdp", None, "tp"),
            P(None, "tp"),
            P("tp", "fsdp"),
            P(),
            P(None, "fsdp", "tp"),
            P("tp", "fsdp"),
        ),
        check_vma=False,
    )
```

```python
import jax
import jax.numpy as jnp
from jax import lax
from jax.sharding import PartitionSpec as P

EPSILON = 1e-05
BF = jnp.bfloat16
F32 = jnp.float32
NX, NY = 4, 4
ROWS = 192


def x_shift(v, d):
    return lax.ppermute(v, "tp", [(i, (i + d) % NX) for i in range(NX)])


def y_shift(v, d):
    route = []
    for f in range(16):
        zh, y, c = f // 8, (f // 2) % 4, f % 2
        route.append((f, zh * 8 + ((y + d) % NY) * 2 + c))
    return lax.ppermute(v, "fsdp", route)


def core_swap(v):
    return lax.ppermute(v, "fsdp", [(f, f ^ 1) for f in range(16)])


def z_cross(v):
    route = []
    for f in range(16):
        for c in range(2):
            route.append((f * 2 + c, (f ^ 8) * 2 + (c ^ 1)))
    return lax.ppermute(v, ("fsdp", "ctx"), route)


def ctx_swap(v):
    return lax.ppermute(v, "ctx", [(0, 1), (1, 0)])


def passed_along(block, distance):
    route = [(0, 1)] if distance == 1 else [(1, 0)]
    return lax.ppermute(block, "ctx", route)


def dot(a, b, dims=(((1,), (0,)), ((), ()))):
    return lax.dot_general(a, b, dims, preferred_element_type=F32)


CC = (((1,), (1,)), ((), ()))
RR = (((0,), (0,)), ((), ()))


def inv_rms_of(v):
    return lax.rsqrt(jnp.mean(v * v, axis=-1, keepdims=True) + EPSILON)


def place(pieces, spots, axis=0):
    size = pieces[0].shape[axis]
    shape = list(pieces[0].shape)
    shape[axis] = size * len(pieces)
    out = jnp.zeros(shape, pieces[0].dtype)
    for piece, spot in zip(pieces, spots):
        out = lax.dynamic_update_slice_in_dim(out, piece, spot * size, axis)
    return out


def block(v, spot, size=ROWS, axis=0):
    return lax.dynamic_slice_in_dim(v, spot * size, size, axis)


def gather_x(v):
    half = v.shape[0] // 2
    down, up = x_shift(v, 1), x_shift(v, -1)
    far = [x_shift(down[:half], 1), x_shift(up[half:], -1)]
    return [v, down, up, jnp.concatenate(far, 0)]


def tie(v, *deps):
    return lax.optimization_barrier((v,) + deps)[0]


def split(v):
    high = v.astype(BF)
    return jnp.concatenate([high, (v - high.astype(F32)).astype(BF)], 0)


def joined(v):
    half = v.shape[0] // 2
    return v[:half].astype(F32) + v[half:].astype(F32)


def tied(values, *deps):
    return list(lax.optimization_barrier(tuple(values) + deps)[: len(values)])


def scatter_x(parts, *deps):
    one, two, three = tied([p.astype(BF) for p in parts[1:]], *deps)
    return [x_shift(three, 2), x_shift(one, -1), x_shift(two, 1)]


def summed(own, got):
    for part in got:
        own = own + part.astype(F32)
    return own


def add_low(a, b):
    return (a.astype(F32) + b.astype(F32)).astype(BF)


def reduce_y(h, note=None):
    own, up, far, down = (h[..., i : i + 128, :] for i in (0, 128, 256, 384))
    near = far[..., :64, :], far[..., 64:, :]
    if note is not None:
        near = [jnp.concatenate([v, note], 0) for v in near]
    from_below, from_above = y_shift(near[0], 1), y_shift(near[1], -1)
    up = jnp.concatenate([add_low(up[..., :64, :], from_below[..., :64, :]), up[..., 64:, :]], -2)
    down = [down[..., :64, :], add_low(down[..., 64:, :], from_above[..., :64, :])]
    if note is not None:
        down.append(from_above[64:])
    down = jnp.concatenate(down, -2)

    def finish():
        one, two = y_shift(up, 1), y_shift(down, -1)
        k = own.astype(F32) + one.astype(F32) + two[..., :128, :].astype(F32)
        notes = [] if note is None else [from_below[64:], from_above[64:], two[128:]]
        return k, notes

    return up, down, finish


def body(
    tokens,
    norm_gain,
    in_weight,
    conv_weight,
    out_weight,
    ffn_gain,
    gate_up_weight,
    down_weight,
    cotangent,
):
    in_shape = tokens.shape
    width = in_shape[-1]
    rows = in_shape[1]
    fi = lax.axis_index("fsdp")
    zh, y, core = fi // 8, (fi // 2) % 4, fi % 2
    x = lax.axis_index("tp")
    spots = [x, (x + 3) % 4, (x + 1) % 4, (x + 2) % 4]
    taps = conv_weight.astype(F32)

    mine = jnp.concatenate([in_weight.reshape(64, 768), out_weight.T], 1)
    pair = jnp.concatenate([mine, z_cross(mine)], 0)
    col = jnp.concatenate([pair, y_shift(pair, -1), y_shift(pair, 2), y_shift(pair, 1)], 0)
    w_mix = jnp.concatenate([col, core_swap(col)], 0)
    w_in = w_mix[:, :768]
    w_out_t = w_mix[:, 768:]

    mine = jnp.concatenate([gate_up_weight, down_weight.T[None]], 0)
    pair = jnp.concatenate([mine, z_cross(mine)], 1)
    above, below = y_shift(pair, -1), y_shift(pair, 1)
    spot = jnp.arange(width)
    blk = spot // 64
    source = ((zh ^ (blk % 2)) * 8 + ((y + blk // 2) % 4) * 2 + (core ^ (blk // 8))) * 64 + spot % 64
    order = (jnp.arange(width)[:, None] == source[None, :]).astype(BF)
    tok = dot(tokens.reshape(-1, width), order).astype(BF)
    cot = dot(cotangent.reshape(-1, width), order).astype(BF)
    both_gains = dot(jnp.stack([norm_gain, ffn_gain], 0), order)
    gain1, gain2 = both_gains[0], both_gains[1]

    x32 = tok.astype(F32)
    inv1 = inv_rms_of(x32)
    normed1 = x32 * inv1
    normed_in = (normed1 * gain1).astype(BF)
    projected = dot(normed_in, w_in)
    gate_b, gate_c, values_v = projected[:, :256], projected[:, 256:512], projected[:, 512:]
    mixed_in = (gate_b * values_v).astype(BF)
    arrived = passed_along(mixed_in[rows - 2 :], 1)
    extended = jnp.concatenate([arrived, mixed_in], 0).astype(F32)
    conv_out = (
        taps[0] * extended[:rows] + taps[1] * extended[1 : rows + 1] + taps[2] * extended[2:]
    )
    gated = (gate_c * conv_out).astype(BF)
    gateds = [block(gated, s) for s in spots]
    own_tok = block(tok, x).astype(F32)
    mixer_parts = [dot(g, w_out_t, CC) for g in gateds]
    middle = summed(own_tok + mixer_parts[0], scatter_x(mixer_parts))

    pair, above, below = tied([pair, above, below], *mixer_parts)
    far = jnp.concatenate([y_shift(above[:, :64], -1), y_shift(below[:, 64:], 1)], 1)
    w_ffn = jnp.zeros((3, width, 1152), BF)
    for slot, piece in ((0, pair), (1, above), (3, below), (2, far)):
        w_ffn = lax.dynamic_update_slice_in_dim(w_ffn, piece, slot * 128, 1)
        w_ffn = lax.dynamic_update_slice_in_dim(w_ffn, core_swap(piece), 512 + slot * 128, 1)
    w_g, w_u, w_dt = w_ffn[0], w_ffn[1], w_ffn[2]

    inv2 = inv_rms_of(middle)
    normed2 = middle * inv2
    nm = gather_x((normed2 * gain2).astype(BF))
    cots = [block(cot, s) for s in spots]
    gates, ups, acts, ffns = [], [], [], []
    for i in range(4):
        if i == 1:
            nm[1:] = tied(nm[1:], ffns[0])
        gates.append(dot(nm[i], w_g))
        ups.append(dot(nm[i], w_u))
        acts.append((gates[i] * jax.nn.sigmoid(gates[i]) * ups[i]).astype(BF))
        ffns.append(dot(acts[i], w_dt, CC))
    got_out = scatter_x(ffns)
    ggs, gus, mids = [None] * 4, [None] * 4, [None] * 4
    for i in (3, 1, 2, 0):
        gate_g, up_u = gates[i], ups[i]
        grad_act = dot(tie(cots[i], *ffns), w_dt)
        sg = jax.nn.sigmoid(gate_g)
        ggs[i] = (grad_act * up_u * sg * (1.0 + gate_g * (1.0 - sg))).astype(BF)
        gus[i] = (grad_act * gate_g * sg).astype(BF)
        mids[i] = dot(ggs[i], w_g, CC) + dot(gus[i], w_u, CC)
    out_rows = summed(tie(middle + ffns[0], *mids), got_out)
    got_mid = scatter_x(mids, out_rows)

    nm_all, cot_all = tied([jnp.concatenate(nm, 0), jnp.concatenate(cots, 0)], out_rows, *mids)
    act_all = jnp.concatenate(acts, 0)
    gg_all = jnp.concatenate(ggs, 0)
    gu_all = jnp.concatenate(gus, 0)

    def ffn_grads(lo):
        n, c = nm_all[:, lo : lo + 512], cot_all[:, lo : lo + 512]
        parts = [dot(n, gg_all, RR), dot(n, gu_all, RR), dot(c, act_all, RR)]
        return jnp.stack([p.astype(BF) for p in parts], 0)

    h_ffn = add_low(ffn_grads(0), core_swap(ffn_grads(512)))
    up_ffn, down_ffn, finish_ffn = reduce_y(h_ffn)
    grad_mid_in = summed(tie(mids[0], h_ffn), got_mid)

    cot_own = cots[0].astype(F32)
    sv = grad_mid_in * gain2
    grad_middle = cot_own + inv2 * (sv - normed2 * jnp.mean(sv * normed2, -1, keepdims=True))
    gain2_part = jnp.sum(grad_mid_in * normed2, 0)
    branches = gather_x(grad_middle.astype(BF))
    branches[3] = tie(branches[3], up_ffn, down_ffn)

    grad_gated = place([dot(p, w_out_t) for p in branches], spots)
    grad_c = grad_gated * conv_out
    grad_conv = grad_gated * gate_c
    back = passed_along(grad_conv[:2], -1)
    padded = jnp.concatenate([grad_conv, back], 0)
    grad_mixed = taps[2] * padded[:rows] + taps[1] * padded[1 : rows + 1] + taps[0] * padded[2:]
    rounded = grad_mixed.astype(BF).astype(F32)
    grad_proj = jnp.concatenate([rounded * values_v, grad_c, rounded * gate_b], 1).astype(BF)
    norm_parts = [dot(block(grad_proj, s), w_in, CC) for s in spots]
    gain1_part = sum(jnp.sum(p * block(normed1, s), 0) for p, s in zip(norm_parts, spots))
    note = split(jnp.stack([gain1_part, gain2_part], 0))
    note = jnp.concatenate([note, jnp.zeros((12, width), BF)], 0)
    sent = tied([jnp.concatenate([p.astype(BF), note], 0) for p in norm_parts[1:]])
    got_rows = [x_shift(sent[2], 2), x_shift(sent[0], -1), x_shift(sent[1], 1)]
    k_ffn, _ = finish_ffn()

    grad_proj_late, branch_all, grad_conv_late = tied(
        [grad_proj, jnp.concatenate(branches, 0), grad_conv], *sent
    )
    gated_all = jnp.concatenate(gateds, 0)
    taps_part = jnp.stack(
        [
            jnp.sum(extended[:rows] * grad_conv_late, 0),
            jnp.sum(extended[1 : rows + 1] * grad_conv_late, 0),
            jnp.sum(extended[2:] * grad_conv_late, 0),
        ],
        0,
    )

    def mix_grads(lo):
        return jnp.concatenate(
            [
                dot(normed_in[:, lo : lo + 512], grad_proj_late, RR),
                dot(branch_all[:, lo : lo + 512], gated_all, RR),
            ],
            1,
        ).astype(BF)

    h_mix = add_low(mix_grads(0), core_swap(mix_grads(512)))
    own_part = tie(norm_parts[0], k_ffn, h_mix, taps_part)
    grad_norm_in = summed(own_part, [g[:192] for g in got_rows])
    gains = joined(note[:4])
    for got in got_rows:
        gains = gains + joined(got[192:196])

    inv1_own = inv_rms_of(own_tok)
    normed1_own = own_tok * inv1_own
    su = grad_norm_in * gain1
    grad_rows = grad_middle + inv1_own * (
        su - normed1_own * jnp.mean(su * normed1_own, -1, keepdims=True)
    )
    both = jnp.concatenate([grad_rows.astype(BF), out_rows.astype(BF)], 0)
    both = gather_x(dot(both, order, CC).astype(BF))
    input_grad = place([v[:ROWS] for v in both], spots).reshape(in_shape)
    result = place([v[ROWS:] for v in both], spots).reshape(in_shape)

    gains = joined(dot(split(gains), order, CC))
    small = jnp.concatenate([gains.reshape(-1), taps_part.reshape(-1), jnp.zeros((256,), F32)], 0)
    small = jnp.concatenate([small.reshape(3, 1024), jnp.zeros((5, 1024), F32)], 0)
    small = small + joined(core_swap(split(small)))
    k, notes = reduce_y(h_mix, split(small))[2]()
    for n in notes:
        small = small + joined(n)
    got = z_cross(jnp.concatenate([k[64:].astype(BF), split(small)], 0))
    half = (k[:64] + got[:64].astype(F32)).astype(BF)
    small = small + joined(got[64:])
    got = ctx_swap(jnp.concatenate([half, split(small)], 0))
    r_mix = half.astype(F32) + got[:64].astype(F32)
    small = small + joined(got[64:])
    half_ffn = add_low(k_ffn[:, :64], z_cross(k_ffn[:, 64:].astype(BF)))
    r_ffn = half_ffn.astype(F32) + ctx_swap(half_ffn).astype(F32)
    return (
        result,
        input_grad,
        small[0],
        r_mix[:, :768].reshape(64, 3, 256),
        small[2, :768].reshape(3, 256),
        r_mix[:, 768:].T,
        small[1],
        r_ffn[:2],
        r_ffn[2].T,
    )


def solution(mesh):
    placed = (
        P("fsdp", "ctx", None),
        P(),
        P("fsdp", None, "tp"),
        P(None, "tp"),
        P("tp", "fsdp"),
        P(),
        P(None, "fsdp", "tp"),
        P("tp", "fsdp"),
        P("fsdp", "ctx", None),
    )
    return jax.shard_map(
        body,
        mesh=mesh,
        in_specs=placed,
        out_specs=(
            P("fsdp", "ctx", None),
            P("fsdp", "ctx", None),
            P(),
            P("fsdp", None, "tp"),
            P(None, "tp"),
            P("tp", "fsdp"),
            P(),
            P(None, "fsdp", "tp"),
            P("tp", "fsdp"),
        ),
        check_vma=False,
    )
```

```python
import functools

import jax
import jax.numpy as jnp
from jax import lax
from jax.experimental import pallas as pl
from jax.experimental.pallas import tpu as pltpu
from jax.sharding import PartitionSpec as P

EPSILON = 1e-05
BF = jnp.bfloat16
F32 = jnp.float32
NX, NY = 4, 4
ROWS = 192


def x_shift(v, d):
    return lax.ppermute(v, "tp", [(i, (i + d) % NX) for i in range(NX)])


def y_shift(v, d):
    route = []
    for f in range(16):
        zh, y, c = f // 8, (f // 2) % 4, f % 2
        route.append((f, zh * 8 + ((y + d) % NY) * 2 + c))
    return lax.ppermute(v, "fsdp", route)


def core_swap(v):
    return lax.ppermute(v, "fsdp", [(f, f ^ 1) for f in range(16)])


def z_cross(v):
    route = []
    for f in range(16):
        for c in range(2):
            route.append((f * 2 + c, (f ^ 8) * 2 + (c ^ 1)))
    return lax.ppermute(v, ("fsdp", "ctx"), route)


def ctx_swap(v):
    return lax.ppermute(v, "ctx", [(0, 1), (1, 0)])


def passed_along(block, distance):
    route = [(0, 1)] if distance == 1 else [(1, 0)]
    return lax.ppermute(block, "ctx", route)


def dot(a, b, dims=(((1,), (0,)), ((), ()))):
    return lax.dot_general(a, b, dims, preferred_element_type=F32)


CC = (((1,), (1,)), ((), ()))
RR = (((0,), (0,)), ((), ()))


def inv_rms_of(v):
    return lax.rsqrt(jnp.mean(v * v, axis=-1, keepdims=True) + EPSILON)


def place(pieces, spots, axis=0):
    size = pieces[0].shape[axis]
    shape = list(pieces[0].shape)
    shape[axis] = size * len(pieces)
    out = jnp.zeros(shape, pieces[0].dtype)
    for piece, spot in zip(pieces, spots):
        out = lax.dynamic_update_slice_in_dim(out, piece, spot * size, axis)
    return out


def block(v, spot, size=ROWS, axis=0):
    return lax.dynamic_slice_in_dim(v, spot * size, size, axis)


def gather_x(v):
    half = v.shape[0] // 2
    down, up = x_shift(v, 1), x_shift(v, -1)
    far = [x_shift(down[:half], 1), x_shift(up[half:], -1)]
    return [v, down, up, jnp.concatenate(far, 0)]


def tie(v, *deps):
    return lax.optimization_barrier((v,) + deps)[0]


def split(v):
    high = v.astype(BF)
    return jnp.concatenate([high, (v - high.astype(F32)).astype(BF)], 0)


def joined(v):
    half = v.shape[0] // 2
    return v[:half].astype(F32) + v[half:].astype(F32)


def tied(values, *deps):
    return list(lax.optimization_barrier(tuple(values) + deps)[: len(values)])


def scatter_x(parts, *deps):
    one, two, three = tied([p.astype(BF) for p in parts[1:]], *deps)
    return [x_shift(three, 2), x_shift(one, -1), x_shift(two, 1)]


def summed(own, got):
    for part in got:
        own = own + part.astype(F32)
    return own


def add_low(a, b):
    return (a.astype(F32) + b.astype(F32)).astype(BF)


def reduce_y(h, note=None):
    own, up, far, down = (h[..., i : i + 128, :] for i in (0, 128, 256, 384))
    near = far[..., :64, :], far[..., 64:, :]
    if note is not None:
        near = [jnp.concatenate([v, note], 0) for v in near]
    from_below, from_above = y_shift(near[0], 1), y_shift(near[1], -1)
    up = jnp.concatenate([add_low(up[..., :64, :], from_below[..., :64, :]), up[..., 64:, :]], -2)
    down = [down[..., :64, :], add_low(down[..., 64:, :], from_above[..., :64, :])]
    if note is not None:
        down.append(from_above[64:])
    down = jnp.concatenate(down, -2)

    one, two = y_shift(up, 1), y_shift(down, -1)

    def finish(*deps):
        one_, two_ = tied([one, two], *deps)
        k = own.astype(F32) + one_.astype(F32) + two_[..., :128, :].astype(F32)
        notes = [] if note is None else [from_below[64:], from_above[64:], two_[128:]]
        return k, notes

    return up, down, finish


IN_VMEM = pl.BlockSpec(memory_space=pltpu.VMEM)
TILES = [(a, min(a + 256, 1152)) for a in range(0, 1152, 256)]


def local_call(kernel, outs, args, scratch=()):
    return pl.pallas_call(
        kernel,
        out_shape=[jax.ShapeDtypeStruct(shape, dtype) for shape, dtype in outs],
        in_specs=[IN_VMEM] * len(args),
        out_specs=[IN_VMEM] * len(outs),
        scratch_shapes=list(scratch),
        compiler_params=pltpu.CompilerParams(vmem_limit_bytes=8 * 2**20),
        cost_estimate=pl.CostEstimate(flops=1024, bytes_accessed=1024, transcendentals=0),
    )(*args)


def mark(v, *refs):
    refs[-1][...] = v[...]


def paced(v, us, *deps):
    return pl.pallas_call(
        mark,
        out_shape=jax.ShapeDtypeStruct(v.shape, v.dtype),
        in_specs=[IN_VMEM] + [pl.BlockSpec(memory_space=pl.ANY)] * len(deps),
        out_specs=IN_VMEM,
        compiler_params=pltpu.CompilerParams(vmem_limit_bytes=2**20),
        cost_estimate=pl.CostEstimate(
            flops=us * 10**9, bytes_accessed=us * 3 * 10**6, transcendentals=0
        ),
    )(v, *deps)


def ffn_forward(*refs):
    pieces, w = refs[:4], refs[4]
    nm, gate, up, act = refs[5:9]
    outs = refs[9:13]
    for i in range(4):
        nm[i * ROWS : (i + 1) * ROWS, :] = pieces[i][...]
    for a, b in TILES:
        gate_g = dot(nm[...], w[0, :, a:b])
        up_u = dot(nm[...], w[1, :, a:b])
        gate[:, a:b] = gate_g
        up[:, a:b] = up_u
        act[:, a:b] = (gate_g * (1.0 / (1.0 + jnp.exp(-gate_g))) * up_u).astype(BF)
    for a in range(0, 1024, 256):
        part = dot(act[...], w[2, a : a + 256, :], CC)
        for i in range(4):
            outs[i][:, a : a + 256] = part[i * ROWS : (i + 1) * ROWS].astype(outs[i].dtype)


def ffn_back(gate, up, nm, cot, act, w, send, keep, *rest):
    mids, gg, gu = rest[:4], rest[4], rest[5]
    for a, b in TILES:
        grad_act = dot(cot[...], w[2, :, a:b])
        gate_g = gate[:, a:b]
        sg = 1.0 / (1.0 + jnp.exp(-gate_g))
        gg[:, a:b] = (grad_act * up[:, a:b] * sg * (1.0 + gate_g * (1.0 - sg))).astype(BF)
        gu[:, a:b] = (grad_act * (gate_g * sg)).astype(BF)
    for a in range(0, 1024, 256):
        part = dot(gg[...], w[0, a : a + 256, :], CC) + dot(gu[...], w[1, a : a + 256, :], CC)
        for i in range(4):
            mids[i][:, a : a + 256] = part[i * ROWS : (i + 1) * ROWS].astype(mids[i].dtype)
    for out, lo in ((send, 512), (keep, 0)):
        for k, left, right in ((0, nm, gg), (1, nm, gu), (2, cot, act)):
            for a, b in TILES:
                out[k, :, a:b] = dot(left[:, lo : lo + 512], right[:, a:b], RR).astype(BF)


def last_rows(own, one, two, three, grad_middle, tok, gain, order, done, out):
    total = own[...] + one[:ROWS].astype(F32) + two[:ROWS].astype(F32) + three[:ROWS].astype(F32)
    inv = lax.rsqrt(jnp.mean(tok[...] * tok[...], axis=-1, keepdims=True) + EPSILON)
    normed = tok[...] * inv
    su = total * gain[...]
    rows = grad_middle[...] + inv * (su - normed * jnp.mean(su * normed, -1, keepdims=True))
    out[:ROWS, :] = dot(rows.astype(BF), order[...], CC).astype(BF)
    out[ROWS:, :] = done[...]


def mix_grads(normed, proj, branch, gated, send, keep):
    for out, lo in ((send, 512), (keep, 0)):
        for a in range(0, 768, 256):
            out[:, a : a + 256] = dot(
                normed[:, lo : lo + 512], proj[:, a : a + 256], RR
            ).astype(BF)
        out[:, 768:] = dot(branch[:, lo : lo + 512], gated[...], RR).astype(BF)


def body(
    tokens,
    norm_gain,
    in_weight,
    conv_weight,
    out_weight,
    ffn_gain,
    gate_up_weight,
    down_weight,
    cotangent,
):
    in_shape = tokens.shape
    width = in_shape[-1]
    rows = in_shape[1]
    fi = lax.axis_index("fsdp")
    zh, y, core = fi // 8, (fi // 2) % 4, fi % 2
    x = lax.axis_index("tp")
    spots = [x, (x + 3) % 4, (x + 1) % 4, (x + 2) % 4]
    taps = conv_weight.astype(F32)

    ffn_mine = jnp.concatenate([gate_up_weight, down_weight.T[None]], 0)
    ffn_pair = jnp.concatenate([ffn_mine, z_cross(ffn_mine)], 1)
    mine = jnp.concatenate([in_weight.reshape(64, 768), out_weight.T], 1)
    pair = jnp.concatenate([mine, z_cross(mine)], 0)
    col = jnp.concatenate([pair, y_shift(pair, -1), y_shift(pair, 2), y_shift(pair, 1)], 0)
    w_mix = jnp.concatenate([col, core_swap(col)], 0)
    w_in = w_mix[:, :768]
    w_out_t = w_mix[:, 768:]

    above, below = y_shift(ffn_pair, -1), y_shift(ffn_pair, 1)
    spot = jnp.arange(width)
    blk = spot // 64
    source = ((zh ^ (blk % 2)) * 8 + ((y + blk // 2) % 4) * 2 + (core ^ (blk // 8))) * 64 + spot % 64
    order = (jnp.arange(width)[:, None] == source[None, :]).astype(BF)
    tok = dot(tie(tokens.reshape(-1, width), pair), order).astype(BF)
    both_gains = dot(jnp.stack([norm_gain, ffn_gain], 0), order)
    gain1, gain2 = both_gains[0], both_gains[1]

    x32 = tok.astype(F32)
    inv1 = inv_rms_of(x32)
    normed1 = x32 * inv1
    normed_in = (normed1 * gain1).astype(BF)
    projected = dot(normed_in, w_in)
    gate_b, gate_c, values_v = projected[:, :256], projected[:, 256:512], projected[:, 512:]
    mixed_in = (gate_b * values_v).astype(BF)
    arrived = passed_along(mixed_in[rows - 2 :], 1)
    extended = jnp.concatenate([arrived, mixed_in], 0).astype(F32)
    conv_out = (
        taps[0] * extended[:rows] + taps[1] * extended[1 : rows + 1] + taps[2] * extended[2:]
    )
    gated = (gate_c * conv_out).astype(BF)
    gateds = [block(gated, s) for s in spots]
    own_tok = block(tok, x).astype(F32)
    mixer_parts = [dot(g, w_out_t, CC) for g in gateds]
    own_part = tie(own_tok + mixer_parts[0], above, below)
    middle = summed(own_part, scatter_x(mixer_parts))

    cot = dot(tie(cotangent.reshape(-1, width), *mixer_parts), order).astype(BF)

    pair, above, below = tied([ffn_pair, above, below], *mixer_parts)
    far = jnp.concatenate([y_shift(above[:, :64], -1), y_shift(below[:, 64:], 1)], 1)
    inv2 = inv_rms_of(middle)
    normed2 = middle * inv2
    nm = gather_x((normed2 * gain2).astype(BF))
    far = tie(far, nm[1], nm[2])
    w_ffn = jnp.zeros((3, width, 1152), BF)
    for slot, piece in ((0, pair), (1, above), (3, below), (2, far)):
        w_ffn = lax.dynamic_update_slice_in_dim(w_ffn, piece, slot * 128, 1)
        w_ffn = lax.dynamic_update_slice_in_dim(w_ffn, core_swap(piece), 512 + slot * 128, 1)

    cots = [block(cot, s) for s in spots]
    piece, hidden = (ROWS, width), (rows, 1152)
    pieces = [(piece, F32), (piece, BF), (piece, BF), (piece, BF)]
    nm_all, gates, ups, act_all, *ffns = local_call(
        ffn_forward,
        [((rows, width), BF), (hidden, F32), (hidden, F32), (hidden, BF), *pieces],
        [*nm, w_ffn],
    )
    got_out = scatter_x(ffns)
    cot_all = tie(jnp.concatenate(cots, 0), *ffns)
    half = ((3, 512, 1152), BF)
    g_send, g_keep, *mids = local_call(
        ffn_back,
        [half, half, *pieces],
        [gates, ups, nm_all, cot_all, act_all, w_ffn],
        [pltpu.VMEM(hidden, BF), pltpu.VMEM(hidden, BF)],
    )
    out_rows = summed(tie(middle + ffns[0], *mids), got_out)
    got_mid = scatter_x(mids, out_rows)

    h_ffn = add_low(g_keep, core_swap(tie(g_send, out_rows)))
    up_ffn, down_ffn, finish_ffn = reduce_y(h_ffn)
    grad_mid_in = summed(mids[0], got_mid)

    cot_own = cots[0].astype(F32)
    sv = grad_mid_in * gain2
    grad_middle = cot_own + inv2 * (sv - normed2 * jnp.mean(sv * normed2, -1, keepdims=True))
    gain2_part = jnp.sum(grad_mid_in * normed2, 0)
    mine = grad_middle.astype(BF)
    branches = [mine, x_shift(mine, 1), x_shift(mine, -1), x_shift(mine, 2)]
    out_rows = dot(out_rows.astype(BF), order, CC).astype(BF)

    grad_gated = place([dot(p, w_out_t) for p in branches], spots)
    grad_c = grad_gated * conv_out
    grad_conv = grad_gated * gate_c
    back = tie(passed_along(grad_conv[:2], -1), up_ffn, down_ffn)
    padded = jnp.concatenate([grad_conv, back], 0)
    grad_mixed = taps[2] * padded[:rows] + taps[1] * padded[1 : rows + 1] + taps[0] * padded[2:]
    rounded = grad_mixed.astype(BF).astype(F32)
    grad_proj = jnp.concatenate([rounded * values_v, grad_c, rounded * gate_b], 1).astype(BF)
    norm_parts = [dot(block(grad_proj, s), w_in, CC) for s in spots]
    gain1_part = sum(jnp.sum(p * block(normed1, s), 0) for p, s in zip(norm_parts, spots))
    note = split(jnp.stack([gain1_part, gain2_part], 0))
    note = jnp.concatenate([note, jnp.zeros((12, width), BF)], 0)
    sent = tied([jnp.concatenate([p.astype(BF), note], 0) for p in norm_parts[1:]])
    got_rows = [x_shift(sent[2], 2), x_shift(sent[0], -1), x_shift(sent[1], 1)]

    grad_proj_late, branch_all, grad_conv_late = tied(
        [grad_proj, jnp.concatenate(branches, 0), grad_conv], *sent
    )
    gated_all = jnp.concatenate(gateds, 0)
    taps_part = jnp.stack(
        [
            jnp.sum(extended[:rows] * grad_conv_late, 0),
            jnp.sum(extended[1 : rows + 1] * grad_conv_late, 0),
            jnp.sum(extended[2:] * grad_conv_late, 0),
        ],
        0,
    )

    half = ((512, 1024), BF)
    m_send, m_keep = local_call(
        mix_grads, [half, half], [normed_in, grad_proj_late, branch_all, gated_all]
    )
    m_got = core_swap(m_send)
    own_part = tie(norm_parts[0], m_keep, m_send, taps_part)

    both = local_call(
        last_rows,
        [((2 * ROWS, width), BF)],
        [own_part, *got_rows, grad_middle, own_tok, gain1[None], order, out_rows],
    )[0]
    after = paced(got_rows[0][192:], 12, both)
    notes = tied([after, got_rows[1][192:], got_rows[2][192:]], after)
    k_ffn = finish_ffn(after)[0]
    m_keep, m_got = tied([m_keep, m_got], after)
    both = gather_x(both)
    both[0] = tie(both[0], both[1])
    input_grad = place([v[:ROWS] for v in both], spots).reshape(in_shape)
    result = place([v[ROWS:] for v in both], spots).reshape(in_shape)

    h_mix = add_low(m_keep, m_got)
    gains = joined(note[:4]) + sum(joined(n[:4]) for n in notes)
    gains = joined(dot(split(gains), order, CC))
    small = jnp.concatenate([gains.reshape(-1), taps_part.reshape(-1), jnp.zeros((256,), F32)], 0)
    small = jnp.concatenate([small.reshape(3, 1024), jnp.zeros((5, 1024), F32)], 0)
    small = small + joined(core_swap(split(small)))
    k, notes = reduce_y(h_mix, split(small))[2]()
    for n in notes:
        small = small + joined(n)
    k = tie(k, both[1], both[2])
    got = z_cross(jnp.concatenate([k[64:].astype(BF), split(small)], 0))
    half = (k[:64] + got[:64].astype(F32)).astype(BF)
    small = small + joined(got[64:])
    got = ctx_swap(jnp.concatenate([half, split(small)], 0))
    r_mix = half.astype(F32) + got[:64].astype(F32)
    small = small + joined(got[64:])
    half_ffn = add_low(k_ffn[:, :64], z_cross(k_ffn[:, 64:].astype(BF)))
    half_ffn = paced(half_ffn, 6, half_ffn)
    got_ffn = ctx_swap(half_ffn)
    return (
        result,
        input_grad,
        small[0],
        r_mix[:, :768].reshape(64, 3, 256),
        small[2, :768].reshape(3, 256),
        r_mix[:, 768:].T,
        small[1],
        half_ffn[:2].astype(F32) + got_ffn[:2].astype(F32),
        (half_ffn[2].astype(F32) + got_ffn[2].astype(F32)).T,
    )


def solution(mesh):
    placed = (
        P("fsdp", "ctx", None),
        P(),
        P("fsdp", None, "tp"),
        P(None, "tp"),
        P("tp", "fsdp"),
        P(),
        P(None, "fsdp", "tp"),
        P("tp", "fsdp"),
        P("fsdp", "ctx", None),
    )
    return jax.shard_map(
        body,
        mesh=mesh,
        in_specs=placed,
        out_specs=(
            P("fsdp", "ctx", None),
            P("fsdp", "ctx", None),
            P(),
            P("fsdp", None, "tp"),
            P(None, "tp"),
            P("tp", "fsdp"),
            P(),
            P(None, "fsdp", "tp"),
            P("tp", "fsdp"),
        ),
        check_vma=False,
    )
```

```python
import functools

import jax
import jax.numpy as jnp
from jax import lax
from jax.experimental import pallas as pl
from jax.experimental.pallas import tpu as pltpu
from jax.sharding import PartitionSpec as P

EPSILON = 1e-05
BF = jnp.bfloat16
F32 = jnp.float32
NX, NY = 4, 4
ROWS = 192


def x_shift(v, d):
    return lax.ppermute(v, "tp", [(i, (i + d) % NX) for i in range(NX)])


def y_shift(v, d):
    route = []
    for f in range(16):
        zh, y, c = f // 8, (f // 2) % 4, f % 2
        route.append((f, zh * 8 + ((y + d) % NY) * 2 + c))
    return lax.ppermute(v, "fsdp", route)


def core_swap(v):
    return lax.ppermute(v, "fsdp", [(f, f ^ 1) for f in range(16)])


def z_cross(v):
    route = []
    for f in range(16):
        for c in range(2):
            route.append((f * 2 + c, (f ^ 8) * 2 + (c ^ 1)))
    return lax.ppermute(v, ("fsdp", "ctx"), route)


def ctx_swap(v):
    return lax.ppermute(v, "ctx", [(0, 1), (1, 0)])


def passed_along(block, distance):
    route = [(0, 1)] if distance == 1 else [(1, 0)]
    return lax.ppermute(block, "ctx", route)


def dot(a, b, dims=(((1,), (0,)), ((), ()))):
    return lax.dot_general(a, b, dims, preferred_element_type=F32)


CC = (((1,), (1,)), ((), ()))
RR = (((0,), (0,)), ((), ()))


def inv_rms_of(v):
    return lax.rsqrt(jnp.mean(v * v, axis=-1, keepdims=True) + EPSILON)


def place(pieces, spots, axis=0):
    size = pieces[0].shape[axis]
    shape = list(pieces[0].shape)
    shape[axis] = size * len(pieces)
    out = jnp.zeros(shape, pieces[0].dtype)
    for piece, spot in zip(pieces, spots):
        out = lax.dynamic_update_slice_in_dim(out, piece, spot * size, axis)
    return out


def block(v, spot, size=ROWS, axis=0):
    return lax.dynamic_slice_in_dim(v, spot * size, size, axis)


def gather_x(v):
    half = v.shape[0] // 2
    down, up = x_shift(v, 1), x_shift(v, -1)
    far = [x_shift(down[:half], 1), x_shift(up[half:], -1)]
    return [v, down, up, jnp.concatenate(far, 0)]


def tie(v, *deps):
    return lax.optimization_barrier((v,) + deps)[0]


def split(v):
    high = v.astype(BF)
    return jnp.concatenate([high, (v - high.astype(F32)).astype(BF)], 0)


def joined(v):
    half = v.shape[0] // 2
    return v[:half].astype(F32) + v[half:].astype(F32)


def tied(values, *deps):
    return list(lax.optimization_barrier(tuple(values) + deps)[: len(values)])


def scatter_x(parts, *deps):
    one, two, three = tied([p.astype(BF) for p in parts[1:]], *deps)
    return [x_shift(three, 2), x_shift(one, -1), x_shift(two, 1)]


def summed(own, got):
    for part in got:
        own = own + part.astype(F32)
    return own


def add_low(a, b):
    return (a.astype(F32) + b.astype(F32)).astype(BF)


def reduce_y(h, note=None):
    own, up, far, down = (h[..., i : i + 128, :] for i in (0, 128, 256, 384))
    near = far[..., :64, :], far[..., 64:, :]
    if note is not None:
        near = [jnp.concatenate([v, note], 0) for v in near]
    from_below, from_above = y_shift(near[0], 1), y_shift(near[1], -1)
    up = jnp.concatenate([add_low(up[..., :64, :], from_below[..., :64, :]), up[..., 64:, :]], -2)
    down = [down[..., :64, :], add_low(down[..., 64:, :], from_above[..., :64, :])]
    if note is not None:
        down.append(from_above[64:])
    down = jnp.concatenate(down, -2)

    one, two = y_shift(up, 1), y_shift(down, -1)

    def finish(*deps):
        one_, two_ = tied([one, two], *deps)
        k = own.astype(F32) + one_.astype(F32) + two_[..., :128, :].astype(F32)
        notes = [] if note is None else [from_below[64:], from_above[64:], two_[128:]]
        return k, notes

    return up, down, finish


IN_VMEM = pl.BlockSpec(memory_space=pltpu.VMEM)
TILES = [(a, min(a + 256, 1152)) for a in range(0, 1152, 256)]


def local_call(kernel, outs, args, first=pltpu.VMEM):
    return pl.pallas_call(
        kernel,
        out_shape=[jax.ShapeDtypeStruct(shape, dtype) for shape, dtype in outs],
        in_specs=[pl.BlockSpec(memory_space=first)] + [IN_VMEM] * (len(args) - 1),
        out_specs=[IN_VMEM] * len(outs),
        compiler_params=pltpu.CompilerParams(vmem_limit_bytes=8 * 2**20),
        cost_estimate=pl.CostEstimate(flops=1024, bytes_accessed=1024, transcendentals=0),
    )(*args)


def mark(v, *refs):
    refs[-1][...] = v[...]


def paced(v, us, *deps):
    return pl.pallas_call(
        mark,
        out_shape=jax.ShapeDtypeStruct(v.shape, v.dtype),
        in_specs=[IN_VMEM] + [pl.BlockSpec(memory_space=pl.ANY)] * len(deps),
        out_specs=IN_VMEM,
        compiler_params=pltpu.CompilerParams(vmem_limit_bytes=2**20),
        cost_estimate=pl.CostEstimate(
            flops=us * 10**9, bytes_accessed=us * 3 * 10**6, transcendentals=0
        ),
    )(v, *deps)


def ffn_forward(*refs):
    pieces, w = refs[:4], refs[4]
    nm, gate, up, act = refs[5:9]
    outs = refs[9:13]
    for i in range(4):
        nm[i * ROWS : (i + 1) * ROWS, :] = pieces[i][...]
    for a, b in TILES:
        gate_g = dot(nm[...], w[0, :, a:b])
        up_u = dot(nm[...], w[1, :, a:b])
        gate[:, a:b] = gate_g
        up[:, a:b] = up_u
        act[:, a:b] = (gate_g * (1.0 / (1.0 + jnp.exp(-gate_g))) * up_u).astype(BF)
    for a in range(0, 1024, 256):
        part = dot(act[...], w[2, a : a + 256, :], CC)
        for i in range(4):
            outs[i][:, a : a + 256] = part[i * ROWS : (i + 1) * ROWS].astype(outs[i].dtype)


def ffn_back(gate, up, nm, cot, act, w, send, gg, gu, *mids):
    for a, b in TILES:
        grad_act = dot(cot[...], w[2, :, a:b])
        gate_g = gate[:, a:b]
        sg = 1.0 / (1.0 + jnp.exp(-gate_g))
        gg[:, a:b] = (grad_act * up[:, a:b] * sg * (1.0 + gate_g * (1.0 - sg))).astype(BF)
        gu[:, a:b] = (grad_act * (gate_g * sg)).astype(BF)
    for a in range(0, 1024, 256):
        part = dot(gg[...], w[0, a : a + 256, :], CC) + dot(gu[...], w[1, a : a + 256, :], CC)
        for i in range(4):
            mids[i][:, a : a + 256] = part[i * ROWS : (i + 1) * ROWS].astype(mids[i].dtype)
    ffn_grads(512, nm, cot, gg, gu, act, send)


def ffn_grads(lo, nm, cot, gg, gu, act, out):
    for k, left, right in ((0, nm, gg), (1, nm, gu), (2, cot, act)):
        for a, b in TILES:
            out[k, :, a:b] = dot(left[:, lo : lo + 512], right[:, a:b], RR).astype(BF)


def norm_rows(spots, proj, w_mix, tok, gain2, own, one, two, three, note):
    gain1 = jnp.zeros((1, 1024), F32)
    for i, out in ((3, three), (1, one), (2, two), (0, own)):
        span = pl.ds(pl.multiple_of(spots[i] * ROWS, ROWS), ROWS)
        part = dot(proj[span, :], w_mix[:, :768], CC)
        x32 = tok[span, :].astype(F32)
        inv = lax.rsqrt(jnp.mean(x32 * x32, axis=-1, keepdims=True) + EPSILON)
        gain1 += jnp.sum(part * (x32 * inv), axis=0, keepdims=True)
        out[:ROWS, :] = part.astype(out.dtype)
    at = lax.broadcasted_iota(jnp.int32, (16, 1024), 0)
    note[...] = jnp.zeros((16, 1024), BF)
    for k, v in ((0, gain1), (1, gain2[...])):
        high = v.astype(BF).astype(F32)
        now = jnp.where(at == k, high, jnp.where(at == k + 2, v - high, note[...].astype(F32)))
        note[...] = now.astype(BF)
    for out in (one, two, three):
        out[ROWS:, :] = note[...]


def last_rows(own, one, two, three, note, grad_middle, tok, gain, order, done, taps, out, small, low):
    total = own[...]
    notes = note[...].astype(F32)
    for got in (one, two, three):
        total += got[:ROWS].astype(F32)
        notes += got[ROWS:].astype(F32)
    x32 = tok[...].astype(F32)
    inv = lax.rsqrt(jnp.mean(x32 * x32, axis=-1, keepdims=True) + EPSILON)
    normed = x32 * inv
    su = total * gain[...]
    rows = grad_middle[...] + inv * (su - normed * jnp.mean(su * normed, -1, keepdims=True))
    out[:ROWS, :] = dot(rows.astype(BF), order[...], CC).astype(BF)
    out[ROWS:, :] = done[...]
    at = lax.broadcasted_iota(jnp.int32, (8, 1024), 0)
    both = notes[0:2] + notes[2:4]
    high = both.astype(BF)
    rest = (both - high.astype(F32)).astype(BF)
    true = dot(high, order[...], CC) + dot(rest, order[...], CC)
    now = jnp.where(at == 0, true[0:1], jnp.where(at == 1, true[1:2], jnp.where(at == 2, taps[...], 0.0)))
    small[...] = now
    low[0:8, :] = now.astype(BF)
    low[8:16, :] = (now - now.astype(BF).astype(F32)).astype(BF)


def mix_grads(normed, proj, branch, gated, send, keep):
    for out, lo in ((send, 512), (keep, 0)):
        for a in range(0, 768, 256):
            out[:, a : a + 256] = dot(
                normed[:, lo : lo + 512], proj[:, a : a + 256], RR
            ).astype(BF)
        out[:, 768:] = dot(branch[:, lo : lo + 512], gated[...], RR).astype(BF)


def body(
    tokens,
    norm_gain,
    in_weight,
    conv_weight,
    out_weight,
    ffn_gain,
    gate_up_weight,
    down_weight,
    cotangent,
):
    in_shape = tokens.shape
    width = in_shape[-1]
    rows = in_shape[1]
    fi = lax.axis_index("fsdp")
    zh, y, core = fi // 8, (fi // 2) % 4, fi % 2
    x = lax.axis_index("tp")
    spots = [x, (x + 3) % 4, (x + 1) % 4, (x + 2) % 4]
    taps = conv_weight.astype(F32)

    ffn_mine = jnp.concatenate([gate_up_weight, down_weight.T[None]], 0)
    ffn_pair = jnp.concatenate([ffn_mine, z_cross(ffn_mine)], 1)
    mine = jnp.concatenate([in_weight.reshape(64, 768), out_weight.T], 1)
    pair = jnp.concatenate([mine, z_cross(mine)], 0)
    col = jnp.concatenate([pair, y_shift(pair, -1), y_shift(pair, 2), y_shift(pair, 1)], 0)
    w_mix = jnp.concatenate([col, core_swap(col)], 0)
    w_in = w_mix[:, :768]
    w_out_t = w_mix[:, 768:]

    above, below = y_shift(ffn_pair, -1), y_shift(ffn_pair, 1)
    spot = jnp.arange(width)
    blk = spot // 64
    source = ((zh ^ (blk % 2)) * 8 + ((y + blk // 2) % 4) * 2 + (core ^ (blk // 8))) * 64 + spot % 64
    order = (jnp.arange(width)[:, None] == source[None, :]).astype(BF)
    tok = dot(tie(tokens.reshape(-1, width), pair), order).astype(BF)
    both_gains = dot(jnp.stack([norm_gain, ffn_gain], 0), order)
    gain1, gain2 = both_gains[0], both_gains[1]

    x32 = tok.astype(F32)
    inv1 = inv_rms_of(x32)
    normed1 = x32 * inv1
    normed_in = (normed1 * gain1).astype(BF)
    projected = dot(normed_in, w_in)
    gate_b, gate_c, values_v = projected[:, :256], projected[:, 256:512], projected[:, 512:]
    mixed_in = (gate_b * values_v).astype(BF)
    arrived = passed_along(mixed_in[rows - 2 :], 1)
    extended = jnp.concatenate([arrived, mixed_in], 0).astype(F32)
    conv_out = (
        taps[0] * extended[:rows] + taps[1] * extended[1 : rows + 1] + taps[2] * extended[2:]
    )
    gated = (gate_c * conv_out).astype(BF)
    gateds = [block(gated, s) for s in spots]
    own_tok = block(tok, x)
    mixer_parts = [dot(g, w_out_t, CC) for g in gateds]
    own_part = tie(own_tok.astype(F32) + mixer_parts[0], above, below)
    middle = summed(own_part, scatter_x(mixer_parts))

    cot = dot(tie(cotangent.reshape(-1, width), *mixer_parts), order).astype(BF)

    above_2, below_2 = tied([above, below], *mixer_parts)
    far = jnp.concatenate([y_shift(above_2[:, :64], -1), y_shift(below_2[:, 64:], 1)], 1)
    inv2 = inv_rms_of(middle)
    normed2 = middle * inv2
    nm = gather_x((normed2 * gain2).astype(BF))
    pair, above, below, far = tied([ffn_pair, above, below, far], nm[1], nm[2])
    w_ffn = jnp.zeros((3, width, 1152), BF)
    for slot, piece in ((0, pair), (1, above), (3, below), (2, far)):
        w_ffn = lax.dynamic_update_slice_in_dim(w_ffn, piece, slot * 128, 1)
        w_ffn = lax.dynamic_update_slice_in_dim(w_ffn, core_swap(piece), 512 + slot * 128, 1)

    cots = [block(cot, s) for s in spots]
    cot_all = jnp.concatenate(cots, 0)
    nm[3] = tie(nm[3], cot_all)
    piece, hidden = (ROWS, width), (rows, 1152)
    pieces = [(piece, F32), (piece, BF), (piece, BF), (piece, BF)]
    nm_all, gates, ups, act_all, *ffns = local_call(
        ffn_forward,
        [((rows, width), BF), (hidden, F32), (hidden, F32), (hidden, BF), *pieces],
        [*nm, w_ffn],
    )
    got_out = scatter_x(ffns)
    cot_all = tie(cot_all, *ffns)
    half = ((3, 512, 1152), BF)
    g_send, gg_all, gu_all, *mids = local_call(
        ffn_back,
        [half, (hidden, BF), (hidden, BF), *pieces],
        [gates, ups, nm_all, cot_all, act_all, w_ffn],
    )
    out_rows = summed(tie(middle + ffns[0], *mids), got_out)
    got_mid = scatter_x(mids, out_rows)

    g_keep = local_call(
        functools.partial(ffn_grads, 0),
        [half],
        [tie(nm_all, out_rows), cot_all, gg_all, gu_all, act_all],
    )[0]
    h_ffn = add_low(g_keep, core_swap(tie(g_send, out_rows)))
    up_ffn, down_ffn, finish_ffn = reduce_y(h_ffn)
    out_rows = dot(out_rows.astype(BF), order, CC).astype(BF)
    grad_mid_in = summed(tie(mids[0], h_ffn, out_rows), got_mid)

    cot_own = cots[0].astype(F32)
    sv = grad_mid_in * gain2
    grad_middle = cot_own + inv2 * (sv - normed2 * jnp.mean(sv * normed2, -1, keepdims=True))
    gain2_part = jnp.sum(grad_mid_in * normed2, 0)
    mine = grad_middle.astype(BF)
    branches = [mine, x_shift(mine, 1), x_shift(mine, -1), x_shift(mine, 2)]

    grad_gated = place([dot(p, w_out_t) for p in branches], spots)
    grad_c = grad_gated * conv_out
    grad_conv = grad_gated * gate_c
    back = tie(passed_along(grad_conv[:2], -1), up_ffn, down_ffn)
    padded = jnp.concatenate([grad_conv, back], 0)
    grad_mixed = taps[2] * padded[:rows] + taps[1] * padded[1 : rows + 1] + taps[0] * padded[2:]
    rounded = grad_mixed.astype(BF).astype(F32)
    grad_proj = jnp.concatenate([rounded * values_v, grad_c, rounded * gate_b], 1).astype(BF)
    longer = ((ROWS + 16, width), BF)
    own_part, *sent, note = local_call(
        norm_rows,
        [(piece, F32), longer, longer, longer, ((16, width), BF)],
        [jnp.stack(spots).astype(jnp.int32), grad_proj, w_mix, tok, gain2_part[None]],
        first=pltpu.SMEM,
    )
    got_rows = [x_shift(sent[2], 2), x_shift(sent[0], -1), x_shift(sent[1], 1)]

    grad_proj_late, branch_all, grad_conv_late = tied(
        [grad_proj, jnp.concatenate(branches, 0), grad_conv], *sent
    )
    gated_all = jnp.concatenate(gateds, 0)
    taps_part = jnp.stack(
        [
            jnp.sum(extended[:rows] * grad_conv_late, 0),
            jnp.sum(extended[1 : rows + 1] * grad_conv_late, 0),
            jnp.sum(extended[2:] * grad_conv_late, 0),
        ],
        0,
    )

    half = ((512, 1024), BF)
    m_send, m_keep = local_call(
        mix_grads, [half, half], [normed_in, grad_proj_late, branch_all, gated_all]
    )
    m_got = core_swap(m_send)
    taps_row = jnp.concatenate([taps_part[0], taps_part[1], taps_part[2], jnp.zeros((256,), F32)])[None]
    own_part = tie(own_part, m_keep, m_send, taps_row)

    both, small, small_low = local_call(
        last_rows,
        [((2 * ROWS, width), BF), ((8, width), F32), ((16, width), BF)],
        [
            own_part,
            *got_rows,
            note,
            grad_middle,
            own_tok,
            gain1[None],
            order,
            out_rows,
            taps_row,
        ],
    )
    after = paced(small_low, 12, both)
    k_ffn = finish_ffn(after)[0]
    m_keep, m_got = tied([m_keep, m_got], after)
    h_mix = add_low(m_keep, m_got)
    both = gather_x(both)
    both[0] = tie(both[0], both[1])
    input_grad = place([v[:ROWS] for v in both], spots).reshape(in_shape)
    result = place([v[ROWS:] for v in both], spots).reshape(in_shape)

    small = small + joined(core_swap(after))
    k, notes = reduce_y(h_mix, split(small))[2]()
    for n in notes:
        small = small + joined(n)
    k = tie(k, both[1], both[2])
    got = z_cross(jnp.concatenate([k[64:].astype(BF), split(small)], 0))
    half = (k[:64] + got[:64].astype(F32)).astype(BF)
    small = small + joined(got[64:])
    got = ctx_swap(jnp.concatenate([half, split(small)], 0))
    r_mix = half.astype(F32) + got[:64].astype(F32)
    small = small + joined(got[64:])
    half_ffn = add_low(k_ffn[:, :64], z_cross(k_ffn[:, 64:].astype(BF)))
    half_ffn = paced(half_ffn, 6, half_ffn)
    got_ffn = ctx_swap(half_ffn)
    return (
        result,
        input_grad,
        small[0],
        r_mix[:, :768].reshape(64, 3, 256),
        small[2, :768].reshape(3, 256),
        r_mix[:, 768:].T,
        small[1],
        half_ffn[:2].astype(F32) + got_ffn[:2].astype(F32),
        (half_ffn[2].astype(F32) + got_ffn[2].astype(F32)).T,
    )


def solution(mesh):
    placed = (
        P("fsdp", "ctx", None),
        P(),
        P("fsdp", None, "tp"),
        P(None, "tp"),
        P("tp", "fsdp"),
        P(),
        P(None, "fsdp", "tp"),
        P("tp", "fsdp"),
        P("fsdp", "ctx", None),
    )
    return jax.shard_map(
        body,
        mesh=mesh,
        in_specs=placed,
        out_specs=(
            P("fsdp", "ctx", None),
            P("fsdp", "ctx", None),
            P(),
            P("fsdp", None, "tp"),
            P(None, "tp"),
            P("tp", "fsdp"),
            P(),
            P(None, "fsdp", "tp"),
            P("tp", "fsdp"),
        ),
        check_vma=False,
    )
```

```python
import functools

import jax
import jax.numpy as jnp
from jax import lax
from jax.experimental import pallas as pl
from jax.experimental.pallas import tpu as pltpu
from jax.sharding import PartitionSpec as P

EPSILON = 1e-05
BF = jnp.bfloat16
F32 = jnp.float32
NX, NY = 4, 4
ROWS = 192


def x_shift(v, d):
    return lax.ppermute(v, "tp", [(i, (i + d) % NX) for i in range(NX)])


def y_shift(v, d):
    route = []
    for f in range(16):
        zh, y, c = f // 8, (f // 2) % 4, f % 2
        route.append((f, zh * 8 + ((y + d) % NY) * 2 + c))
    return lax.ppermute(v, "fsdp", route)


def core_swap(v):
    return lax.ppermute(v, "fsdp", [(f, f ^ 1) for f in range(16)])


def z_cross(v):
    route = []
    for f in range(16):
        for c in range(2):
            route.append((f * 2 + c, (f ^ 8) * 2 + (c ^ 1)))
    return lax.ppermute(v, ("fsdp", "ctx"), route)


def ctx_swap(v):
    return lax.ppermute(v, "ctx", [(0, 1), (1, 0)])


def passed_along(block, distance):
    route = [(0, 1)] if distance == 1 else [(1, 0)]
    return lax.ppermute(block, "ctx", route)


def dot(a, b, dims=(((1,), (0,)), ((), ()))):
    return lax.dot_general(a, b, dims, preferred_element_type=F32)


CC = (((1,), (1,)), ((), ()))
RR = (((0,), (0,)), ((), ()))


def inv_rms_of(v):
    return lax.rsqrt(jnp.mean(v * v, axis=-1, keepdims=True) + EPSILON)


def place(pieces, spots, axis=0):
    size = pieces[0].shape[axis]
    shape = list(pieces[0].shape)
    shape[axis] = size * len(pieces)
    out = jnp.zeros(shape, pieces[0].dtype)
    for piece, spot in zip(pieces, spots):
        out = lax.dynamic_update_slice_in_dim(out, piece, spot * size, axis)
    return out


def block(v, spot, size=ROWS, axis=0):
    return lax.dynamic_slice_in_dim(v, spot * size, size, axis)


def gather_x(v):
    half = v.shape[0] // 2
    down, up = x_shift(v, 1), x_shift(v, -1)
    far = [x_shift(down[:half], 1), x_shift(up[half:], -1)]
    return [v, down, up, jnp.concatenate(far, 0)]


def tie(v, *deps):
    return lax.optimization_barrier((v,) + deps)[0]


def split(v):
    high = v.astype(BF)
    return jnp.concatenate([high, (v - high.astype(F32)).astype(BF)], 0)


def joined(v):
    half = v.shape[0] // 2
    return v[:half].astype(F32) + v[half:].astype(F32)


def tied(values, *deps):
    return list(lax.optimization_barrier(tuple(values) + deps)[: len(values)])


def scatter_x(parts, *deps):
    one, two, three = tied([p.astype(BF) for p in parts[1:]], *deps)
    return [x_shift(three, 2), x_shift(one, -1), x_shift(two, 1)]


def summed(own, got):
    for part in got:
        own = own + part.astype(F32)
    return own


def add_low(a, b):
    return (a.astype(F32) + b.astype(F32)).astype(BF)


def reduce_y(h, note=None):
    own, up, far, down = (h[..., i : i + 128, :] for i in (0, 128, 256, 384))
    near = far[..., :64, :], far[..., 64:, :]
    if note is not None:
        near = [jnp.concatenate([v, note], 0) for v in near]
    from_below, from_above = y_shift(near[0], 1), y_shift(near[1], -1)
    up = jnp.concatenate([add_low(up[..., :64, :], from_below[..., :64, :]), up[..., 64:, :]], -2)
    down = [down[..., :64, :], add_low(down[..., 64:, :], from_above[..., :64, :])]
    if note is not None:
        down.append(from_above[64:])
    down = jnp.concatenate(down, -2)

    one, two = y_shift(up, 1), y_shift(down, -1)

    def finish(*deps):
        one_, two_ = tied([one, two], *deps)
        k = own.astype(F32) + one_.astype(F32) + two_[..., :128, :].astype(F32)
        notes = [] if note is None else [from_below[64:], from_above[64:], two_[128:]]
        return k, notes

    return up, down, finish


IN_VMEM = pl.BlockSpec(memory_space=pltpu.VMEM)
TILES = [(a, min(a + 256, 1152)) for a in range(0, 1152, 256)]


def local_call(kernel, outs, args, first=pltpu.VMEM):
    return pl.pallas_call(
        kernel,
        out_shape=[jax.ShapeDtypeStruct(shape, dtype) for shape, dtype in outs],
        in_specs=[pl.BlockSpec(memory_space=first)] + [IN_VMEM] * (len(args) - 1),
        out_specs=[IN_VMEM] * len(outs),
        compiler_params=pltpu.CompilerParams(vmem_limit_bytes=8 * 2**20),
        cost_estimate=pl.CostEstimate(flops=1024, bytes_accessed=1024, transcendentals=0),
    )(*args)


def mark(v, *refs):
    refs[-1][...] = v[...]


def paced(v, us, *deps):
    return pl.pallas_call(
        mark,
        out_shape=jax.ShapeDtypeStruct(v.shape, v.dtype),
        in_specs=[IN_VMEM] + [pl.BlockSpec(memory_space=pl.ANY)] * len(deps),
        out_specs=IN_VMEM,
        compiler_params=pltpu.CompilerParams(vmem_limit_bytes=2**20),
        cost_estimate=pl.CostEstimate(
            flops=us * 10**9, bytes_accessed=us * 3 * 10**6, transcendentals=0
        ),
    )(v, *deps)


def ffn_forward(*refs):
    pieces, w = refs[:4], refs[4]
    nm, gate, up, act = refs[5:9]
    outs = refs[9:13]
    for i in range(4):
        nm[i * ROWS : (i + 1) * ROWS, :] = pieces[i][...]
    for a, b in TILES:
        gate_g = dot(nm[...], w[0, :, a:b])
        up_u = dot(nm[...], w[1, :, a:b])
        gate[:, a:b] = gate_g
        up[:, a:b] = up_u
        act[:, a:b] = (gate_g * (1.0 / (1.0 + jnp.exp(-gate_g))) * up_u).astype(BF)
    for a in range(0, 1024, 256):
        part = dot(act[...], w[2, a : a + 256, :], CC)
        for i in range(4):
            outs[i][:, a : a + 256] = part[i * ROWS : (i + 1) * ROWS].astype(outs[i].dtype)


def ffn_back(gate, up, nm, cot, act, w, send, gg, gu, *mids):
    for a, b in TILES:
        grad_act = dot(cot[...], w[2, :, a:b])
        gate_g = gate[:, a:b]
        sg = 1.0 / (1.0 + jnp.exp(-gate_g))
        gg[:, a:b] = (grad_act * up[:, a:b] * sg * (1.0 + gate_g * (1.0 - sg))).astype(BF)
        gu[:, a:b] = (grad_act * (gate_g * sg)).astype(BF)
    for a in range(0, 1024, 256):
        part = dot(gg[...], w[0, a : a + 256, :], CC) + dot(gu[...], w[1, a : a + 256, :], CC)
        for i in range(4):
            mids[i][:, a : a + 256] = part[i * ROWS : (i + 1) * ROWS].astype(mids[i].dtype)
    ffn_grads(512, nm, cot, gg, gu, act, send)


def ffn_grads(lo, nm, cot, gg, gu, act, out):
    for k, left, right in ((0, nm, gg), (1, nm, gu), (2, cot, act)):
        for a, b in TILES:
            out[k, :, a:b] = dot(left[:, lo : lo + 512], right[:, a:b], RR).astype(BF)


def norm_rows(spots, proj, w_mix, tok, gain2, own, one, two, three, note):
    gain1 = jnp.zeros((1, 1024), F32)
    for i, out in ((3, three), (1, one), (2, two), (0, own)):
        span = pl.ds(pl.multiple_of(spots[i] * ROWS, ROWS), ROWS)
        part = dot(proj[span, :], w_mix[:, :768], CC)
        x32 = tok[span, :].astype(F32)
        inv = lax.rsqrt(jnp.mean(x32 * x32, axis=-1, keepdims=True) + EPSILON)
        gain1 += jnp.sum(part * (x32 * inv), axis=0, keepdims=True)
        out[:ROWS, :] = part.astype(out.dtype)
    at = lax.broadcasted_iota(jnp.int32, (16, 1024), 0)
    note[...] = jnp.zeros((16, 1024), BF)
    for k, v in ((0, gain1), (1, gain2[...])):
        high = v.astype(BF).astype(F32)
        now = jnp.where(at == k, high, jnp.where(at == k + 2, v - high, note[...].astype(F32)))
        note[...] = now.astype(BF)
    for out in (one, two, three):
        out[ROWS:, :] = note[...]


def last_rows(own, one, two, three, note, grad_middle, tok, gain, order, done, taps, out, small, low):
    total = own[...]
    notes = note[...].astype(F32)
    for got in (one, two, three):
        total += got[:ROWS].astype(F32)
        notes += got[ROWS:].astype(F32)
    x32 = tok[...].astype(F32)
    inv = lax.rsqrt(jnp.mean(x32 * x32, axis=-1, keepdims=True) + EPSILON)
    normed = x32 * inv
    su = total * gain[...]
    rows = grad_middle[...] + inv * (su - normed * jnp.mean(su * normed, -1, keepdims=True))
    out[:ROWS, :] = dot(rows.astype(BF), order[...], CC).astype(BF)
    out[ROWS:, :] = done[...]
    at = lax.broadcasted_iota(jnp.int32, (8, 1024), 0)
    both = notes[0:2] + notes[2:4]
    high = both.astype(BF)
    rest = (both - high.astype(F32)).astype(BF)
    true = dot(high, order[...], CC) + dot(rest, order[...], CC)
    now = jnp.where(at == 0, true[0:1], jnp.where(at == 1, true[1:2], jnp.where(at == 2, taps[...], 0.0)))
    small[...] = now
    low[0:8, :] = now.astype(BF)
    low[8:16, :] = (now - now.astype(BF).astype(F32)).astype(BF)


def mix_grads(normed, proj, branch, gated, send, keep):
    for out, lo in ((send, 512), (keep, 0)):
        for a in range(0, 768, 256):
            out[:, a : a + 256] = dot(
                normed[:, lo : lo + 512], proj[:, a : a + 256], RR
            ).astype(BF)
        out[:, 768:] = dot(branch[:, lo : lo + 512], gated[...], RR).astype(BF)


def body(
    tokens,
    norm_gain,
    in_weight,
    conv_weight,
    out_weight,
    ffn_gain,
    gate_up_weight,
    down_weight,
    cotangent,
):
    in_shape = tokens.shape
    width = in_shape[-1]
    rows = in_shape[1]
    fi = lax.axis_index("fsdp")
    zh, y, core = fi // 8, (fi // 2) % 4, fi % 2
    x = lax.axis_index("tp")
    spots = [x, (x + 3) % 4, (x + 1) % 4, (x + 2) % 4]
    taps = conv_weight.astype(F32)

    ffn_mine = jnp.concatenate([gate_up_weight, down_weight.T[None]], 0)
    ffn_pair = jnp.concatenate([ffn_mine, z_cross(ffn_mine)], 1)
    mine = jnp.concatenate([in_weight.reshape(64, 768), out_weight.T], 1)
    pair = jnp.concatenate([mine, z_cross(mine)], 0)
    col = jnp.concatenate([pair, y_shift(pair, -1), y_shift(pair, 2), y_shift(pair, 1)], 0)
    w_mix = jnp.concatenate([col, core_swap(col)], 0)
    w_in = w_mix[:, :768]
    w_out_t = w_mix[:, 768:]

    above, below = y_shift(ffn_pair, -1), y_shift(ffn_pair, 1)
    spot = jnp.arange(width)
    blk = spot // 64
    source = ((zh ^ (blk % 2)) * 8 + ((y + blk // 2) % 4) * 2 + (core ^ (blk // 8))) * 64 + spot % 64
    order = (jnp.arange(width)[:, None] == source[None, :]).astype(BF)
    tok = dot(tie(tokens.reshape(-1, width), pair), order).astype(BF)
    both_gains = dot(jnp.stack([norm_gain, ffn_gain], 0), order)
    gain1, gain2 = both_gains[0], both_gains[1]

    x32 = tok.astype(F32)
    inv1 = inv_rms_of(x32)
    normed1 = x32 * inv1
    normed_in = (normed1 * gain1).astype(BF)
    projected = dot(normed_in, w_in)
    gate_b, gate_c, values_v = projected[:, :256], projected[:, 256:512], projected[:, 512:]
    mixed_in = (gate_b * values_v).astype(BF)
    arrived = passed_along(mixed_in[rows - 2 :], 1)
    extended = jnp.concatenate([arrived, mixed_in], 0).astype(F32)
    conv_out = (
        taps[0] * extended[:rows] + taps[1] * extended[1 : rows + 1] + taps[2] * extended[2:]
    )
    gated = (gate_c * conv_out).astype(BF)
    gateds = [block(gated, s) for s in spots]
    own_tok = block(tok, x)
    mixer_parts = [dot(g, w_out_t, CC) for g in gateds]
    own_part = tie(own_tok.astype(F32) + mixer_parts[0], above, below)
    middle = summed(own_part, scatter_x(mixer_parts))

    cot = dot(tie(cotangent.reshape(-1, width), *mixer_parts), order).astype(BF)

    above_2, below_2 = tied([above, below], *mixer_parts)
    far = jnp.concatenate([y_shift(above_2[:, :64], -1), y_shift(below_2[:, 64:], 1)], 1)
    inv2 = inv_rms_of(middle)
    normed2 = middle * inv2
    nm = gather_x((normed2 * gain2).astype(BF))
    pair = ffn_pair
    above, below, far = tied([above, below, far], nm[1], nm[2])
    w_ffn = jnp.zeros((3, width, 1152), BF)
    for slot, piece in ((0, pair), (1, above), (3, below), (2, far)):
        w_ffn = lax.dynamic_update_slice_in_dim(w_ffn, piece, slot * 128, 1)
        w_ffn = lax.dynamic_update_slice_in_dim(w_ffn, core_swap(piece), 512 + slot * 128, 1)

    cots = [block(cot, s) for s in spots]
    cot_all = jnp.concatenate(cots, 0)
    nm[3] = tie(nm[3], cot_all)
    piece, hidden = (ROWS, width), (rows, 1152)
    pieces = [(piece, F32), (piece, BF), (piece, BF), (piece, BF)]
    nm_all, gates, ups, act_all, *ffns = local_call(
        ffn_forward,
        [((rows, width), BF), (hidden, F32), (hidden, F32), (hidden, BF), *pieces],
        [*nm, w_ffn],
    )
    got_out = scatter_x(ffns)
    cot_all = tie(cot_all, *ffns)
    half = ((3, 512, 1152), BF)
    g_send, gg_all, gu_all, *mids = local_call(
        ffn_back,
        [half, (hidden, BF), (hidden, BF), *pieces],
        [gates, ups, nm_all, cot_all, act_all, w_ffn],
    )
    out_rows = summed(tie(middle + ffns[0], *mids), got_out)
    got_mid = scatter_x(mids, out_rows)

    g_keep = local_call(
        functools.partial(ffn_grads, 0),
        [half],
        [tie(nm_all, out_rows), cot_all, gg_all, gu_all, act_all],
    )[0]
    h_ffn = add_low(g_keep, core_swap(tie(g_send, out_rows)))
    up_ffn, down_ffn, finish_ffn = reduce_y(h_ffn)
    out_rows = dot(out_rows.astype(BF), order, CC).astype(BF)
    grad_mid_in = summed(tie(mids[0], h_ffn, out_rows), got_mid)

    cot_own = cots[0].astype(F32)
    sv = grad_mid_in * gain2
    grad_middle = cot_own + inv2 * (sv - normed2 * jnp.mean(sv * normed2, -1, keepdims=True))
    gain2_part = jnp.sum(grad_mid_in * normed2, 0)
    mine = grad_middle.astype(BF)
    branches = [mine, x_shift(mine, 1), x_shift(mine, -1), x_shift(mine, 2)]

    grad_gated = place([dot(p, w_out_t) for p in branches], spots)
    grad_c = grad_gated * conv_out
    grad_conv = grad_gated * gate_c
    back = tie(passed_along(grad_conv[:2], -1), up_ffn, down_ffn)
    padded = jnp.concatenate([grad_conv, back], 0)
    grad_mixed = taps[2] * padded[:rows] + taps[1] * padded[1 : rows + 1] + taps[0] * padded[2:]
    rounded = grad_mixed.astype(BF).astype(F32)
    grad_proj = jnp.concatenate([rounded * values_v, grad_c, rounded * gate_b], 1).astype(BF)
    longer = ((ROWS + 16, width), BF)
    own_part, *sent, note = local_call(
        norm_rows,
        [(piece, F32), longer, longer, longer, ((16, width), BF)],
        [jnp.stack(spots).astype(jnp.int32), grad_proj, w_mix, tok, gain2_part[None]],
        first=pltpu.SMEM,
    )
    got_rows = [x_shift(sent[2], 2), x_shift(sent[0], -1), x_shift(sent[1], 1)]

    grad_proj_late, branch_all, grad_conv_late = tied(
        [grad_proj, jnp.concatenate(branches, 0), grad_conv], *sent
    )
    gated_all = jnp.concatenate(gateds, 0)
    taps_part = jnp.stack(
        [
            jnp.sum(extended[:rows] * grad_conv_late, 0),
            jnp.sum(extended[1 : rows + 1] * grad_conv_late, 0),
            jnp.sum(extended[2:] * grad_conv_late, 0),
        ],
        0,
    )

    half = ((512, 1024), BF)
    m_send, m_keep = local_call(
        mix_grads, [half, half], [normed_in, grad_proj_late, branch_all, gated_all]
    )
    m_got = core_swap(m_send)
    taps_row = jnp.concatenate([taps_part[0], taps_part[1], taps_part[2], jnp.zeros((256,), F32)])[None]
    own_part = tie(own_part, m_keep, m_send, taps_row)

    both, small, small_low = local_call(
        last_rows,
        [((2 * ROWS, width), BF), ((8, width), F32), ((16, width), BF)],
        [
            own_part,
            *got_rows,
            note,
            grad_middle,
            own_tok,
            gain1[None],
            order,
            out_rows,
            taps_row,
        ],
    )
    after = paced(small_low, 12, both)
    k_ffn = finish_ffn(after)[0]
    m_keep, m_got = tied([m_keep, m_got], after)
    h_mix = add_low(m_keep, m_got)
    both = gather_x(both)
    both[0] = tie(both[0], both[1])
    input_grad = place([v[:ROWS] for v in both], spots).reshape(in_shape)
    result = place([v[ROWS:] for v in both], spots).reshape(in_shape)

    small = small + joined(core_swap(after))
    k, notes = reduce_y(h_mix, split(small))[2]()
    for n in notes:
        small = small + joined(n)
    k = tie(k, both[1], both[2])
    got = z_cross(jnp.concatenate([k[64:].astype(BF), split(small)], 0))
    half = (k[:64] + got[:64].astype(F32)).astype(BF)
    small = small + joined(got[64:])
    got = ctx_swap(jnp.concatenate([half, split(small)], 0))
    r_mix = [half[:, a : a + 256].astype(F32) + got[:64, a : a + 256].astype(F32) for a in (0, 256, 512, 768)]
    small = small + joined(got[64:])
    half_ffn = add_low(k_ffn[:, :64], z_cross(k_ffn[:, 64:].astype(BF)))
    half_ffn = paced(half_ffn, 6, half_ffn)
    got_ffn = ctx_swap(half_ffn)
    return (
        result,
        input_grad,
        small[0],
        jnp.stack(r_mix[:3], 1),
        small[2, :768].reshape(3, 256),
        r_mix[3].T,
        small[1],
        half_ffn[:2].astype(F32) + got_ffn[:2].astype(F32),
        (half_ffn[2].astype(F32) + got_ffn[2].astype(F32)).T,
    )


def solution(mesh):
    placed = (
        P("fsdp", "ctx", None),
        P(),
        P("fsdp", None, "tp"),
        P(None, "tp"),
        P("tp", "fsdp"),
        P(),
        P(None, "fsdp", "tp"),
        P("tp", "fsdp"),
        P("fsdp", "ctx", None),
    )
    return jax.shard_map(
        body,
        mesh=mesh,
        in_specs=placed,
        out_specs=(
            P("fsdp", "ctx", None),
            P("fsdp", "ctx", None),
            P(),
            P("fsdp", None, "tp"),
            P(None, "tp"),
            P("tp", "fsdp"),
            P(),
            P(None, "fsdp", "tp"),
            P("tp", "fsdp"),
        ),
        check_vma=False,
    )
```

```python
import functools

import jax
import jax.numpy as jnp
from jax import lax
from jax.experimental import pallas as pl
from jax.experimental.pallas import tpu as pltpu
from jax.sharding import PartitionSpec as P

EPSILON = 1e-05
BF = jnp.bfloat16
F32 = jnp.float32
NX, NY = 4, 4
ROWS = 192


def x_shift(v, d):
    return lax.ppermute(v, "tp", [(i, (i + d) % NX) for i in range(NX)])


def y_shift(v, d):
    route = []
    for f in range(16):
        zh, y, c = f // 8, (f // 2) % 4, f % 2
        route.append((f, zh * 8 + ((y + d) % NY) * 2 + c))
    return lax.ppermute(v, "fsdp", route)


def core_swap(v):
    return lax.ppermute(v, "fsdp", [(f, f ^ 1) for f in range(16)])


def z_cross(v):
    route = []
    for f in range(16):
        for c in range(2):
            route.append((f * 2 + c, (f ^ 8) * 2 + (c ^ 1)))
    return lax.ppermute(v, ("fsdp", "ctx"), route)


def ctx_swap(v):
    return lax.ppermute(v, "ctx", [(0, 1), (1, 0)])


def passed_along(block, distance):
    route = [(0, 1)] if distance == 1 else [(1, 0)]
    return lax.ppermute(block, "ctx", route)


def dot(a, b, dims=(((1,), (0,)), ((), ()))):
    return lax.dot_general(a, b, dims, preferred_element_type=F32)


CC = (((1,), (1,)), ((), ()))
RR = (((0,), (0,)), ((), ()))


def inv_rms_of(v):
    return lax.rsqrt(jnp.mean(v * v, axis=-1, keepdims=True) + EPSILON)


def place(pieces, spots, axis=0):
    size = pieces[0].shape[axis]
    shape = list(pieces[0].shape)
    shape[axis] = size * len(pieces)
    out = jnp.zeros(shape, pieces[0].dtype)
    for piece, spot in zip(pieces, spots):
        out = lax.dynamic_update_slice_in_dim(out, piece, spot * size, axis)
    return out


def block(v, spot, size=ROWS, axis=0):
    return lax.dynamic_slice_in_dim(v, spot * size, size, axis)


def gather_x(v):
    half = v.shape[0] // 2
    down, up = x_shift(v, 1), x_shift(v, -1)
    far = [x_shift(down[:half], 1), x_shift(up[half:], -1)]
    return [v, down, up, jnp.concatenate(far, 0)]


def tie(v, *deps):
    return lax.optimization_barrier((v,) + deps)[0]


def split(v):
    high = v.astype(BF)
    return jnp.concatenate([high, (v - high.astype(F32)).astype(BF)], 0)


def joined(v):
    half = v.shape[0] // 2
    return v[:half].astype(F32) + v[half:].astype(F32)


def tied(values, *deps):
    return list(lax.optimization_barrier(tuple(values) + deps)[: len(values)])


def scatter_x(parts, *deps):
    one, two, three = tied([p.astype(BF) for p in parts[1:]], *deps)
    return [x_shift(three, 2), x_shift(one, -1), x_shift(two, 1)]


def summed(own, got):
    for part in got:
        own = own + part.astype(F32)
    return own


def add_low(a, b):
    return (a.astype(F32) + b.astype(F32)).astype(BF)


def reduce_y(h, note=None):
    own, up, far, down = (h[..., i : i + 128, :] for i in (0, 128, 256, 384))
    near = far[..., :64, :], far[..., 64:, :]
    if note is not None:
        near = [jnp.concatenate([v, note], 0) for v in near]
    from_below, from_above = y_shift(near[0], 1), y_shift(near[1], -1)
    up = jnp.concatenate([add_low(up[..., :64, :], from_below[..., :64, :]), up[..., 64:, :]], -2)
    down = [down[..., :64, :], add_low(down[..., 64:, :], from_above[..., :64, :])]
    if note is not None:
        down.append(from_above[64:])
    down = jnp.concatenate(down, -2)

    one, two = y_shift(up, 1), y_shift(down, -1)

    def finish(*deps):
        one_, two_ = tied([one, two], *deps)
        k = own.astype(F32) + one_.astype(F32) + two_[..., :128, :].astype(F32)
        notes = [] if note is None else [from_below[64:], from_above[64:], two_[128:]]
        return k, notes

    return up, down, finish


IN_VMEM = pl.BlockSpec(memory_space=pltpu.VMEM)
TILES = [(a, min(a + 256, 1152)) for a in range(0, 1152, 256)]


def local_call(kernel, outs, args, first=pltpu.VMEM):
    return pl.pallas_call(
        kernel,
        out_shape=[jax.ShapeDtypeStruct(shape, dtype) for shape, dtype in outs],
        in_specs=[pl.BlockSpec(memory_space=first)] + [IN_VMEM] * (len(args) - 1),
        out_specs=[IN_VMEM] * len(outs),
        compiler_params=pltpu.CompilerParams(vmem_limit_bytes=8 * 2**20),
        cost_estimate=pl.CostEstimate(flops=1024, bytes_accessed=1024, transcendentals=0),
    )(*args)


def mark(v, *refs):
    refs[-1][...] = v[...]


def paced(v, us, *deps):
    return pl.pallas_call(
        mark,
        out_shape=jax.ShapeDtypeStruct(v.shape, v.dtype),
        in_specs=[IN_VMEM] + [pl.BlockSpec(memory_space=pl.ANY)] * len(deps),
        out_specs=IN_VMEM,
        compiler_params=pltpu.CompilerParams(vmem_limit_bytes=2**20),
        cost_estimate=pl.CostEstimate(
            flops=us * 10**9, bytes_accessed=us * 3 * 10**6, transcendentals=0
        ),
    )(v, *deps)


def ffn_forward(*refs):
    pieces, w = refs[:4], refs[4]
    nm, gate, up, act = refs[5:9]
    outs = refs[9:13]
    for i in range(4):
        nm[i * ROWS : (i + 1) * ROWS, :] = pieces[i][...]
    for a, b in TILES:
        gate_g = dot(nm[...], w[0, :, a:b])
        up_u = dot(nm[...], w[1, :, a:b])
        gate[:, a:b] = gate_g
        up[:, a:b] = up_u
        act[:, a:b] = (gate_g * (1.0 / (1.0 + jnp.exp(-gate_g))) * up_u).astype(BF)
    for a in range(0, 1024, 256):
        part = dot(act[...], w[2, a : a + 256, :], CC)
        for i in range(4):
            outs[i][:, a : a + 256] = part[i * ROWS : (i + 1) * ROWS].astype(outs[i].dtype)


def ffn_back(gate, up, nm, cot, act, w, send, gg, gu, *mids):
    for a, b in TILES:
        grad_act = dot(cot[...], w[2, :, a:b])
        gate_g = gate[:, a:b]
        sg = 1.0 / (1.0 + jnp.exp(-gate_g))
        gg[:, a:b] = (grad_act * up[:, a:b] * sg * (1.0 + gate_g * (1.0 - sg))).astype(BF)
        gu[:, a:b] = (grad_act * (gate_g * sg)).astype(BF)
    for a in range(0, 1024, 256):
        part = dot(gg[...], w[0, a : a + 256, :], CC) + dot(gu[...], w[1, a : a + 256, :], CC)
        for i in range(4):
            mids[i][:, a : a + 256] = part[i * ROWS : (i + 1) * ROWS].astype(mids[i].dtype)
    ffn_grads(512, nm, cot, gg, gu, act, send)


def ffn_grads(lo, nm, cot, gg, gu, act, out):
    for k, left, right in ((0, nm, gg), (1, nm, gu), (2, cot, act)):
        for a, b in TILES:
            out[k, :, a:b] = dot(left[:, lo : lo + 512], right[:, a:b], RR).astype(BF)


def norm_rows(spots, proj, w_mix, tok, gain2, own, one, two, three, note):
    gain1 = jnp.zeros((1, 1024), F32)
    for i, out in ((3, three), (1, one), (2, two), (0, own)):
        span = pl.ds(pl.multiple_of(spots[i] * ROWS, ROWS), ROWS)
        part = dot(proj[span, :], w_mix[:, :768], CC)
        x32 = tok[span, :].astype(F32)
        inv = lax.rsqrt(jnp.mean(x32 * x32, axis=-1, keepdims=True) + EPSILON)
        gain1 += jnp.sum(part * (x32 * inv), axis=0, keepdims=True)
        out[:ROWS, :] = part.astype(out.dtype)
    at = lax.broadcasted_iota(jnp.int32, (16, 1024), 0)
    note[...] = jnp.zeros((16, 1024), BF)
    for k, v in ((0, gain1), (1, gain2[...])):
        high = v.astype(BF).astype(F32)
        now = jnp.where(at == k, high, jnp.where(at == k + 2, v - high, note[...].astype(F32)))
        note[...] = now.astype(BF)
    for out in (one, two, three):
        out[ROWS:, :] = note[...]


def last_rows(own, one, two, three, note, grad_middle, tok, gain, order, done, taps, out, small, low):
    total = own[...]
    notes = note[...].astype(F32)
    for got in (one, two, three):
        total += got[:ROWS].astype(F32)
        notes += got[ROWS:].astype(F32)
    x32 = tok[...].astype(F32)
    inv = lax.rsqrt(jnp.mean(x32 * x32, axis=-1, keepdims=True) + EPSILON)
    normed = x32 * inv
    su = total * gain[...]
    rows = grad_middle[...] + inv * (su - normed * jnp.mean(su * normed, -1, keepdims=True))
    out[:ROWS, :] = dot(rows.astype(BF), order[...], CC).astype(BF)
    out[ROWS:, :] = done[...]
    at = lax.broadcasted_iota(jnp.int32, (8, 1024), 0)
    both = notes[0:2] + notes[2:4]
    high = both.astype(BF)
    rest = (both - high.astype(F32)).astype(BF)
    true = dot(high, order[...], CC) + dot(rest, order[...], CC)
    now = jnp.where(at == 0, true[0:1], jnp.where(at == 1, true[1:2], jnp.where(at == 2, taps[...], 0.0)))
    small[...] = now
    low[0:8, :] = now.astype(BF)
    low[8:16, :] = (now - now.astype(BF).astype(F32)).astype(BF)


def mix_grads(normed, proj, branch, gated, send, keep):
    for out, lo in ((send, 512), (keep, 0)):
        for a in range(0, 768, 256):
            out[:, a : a + 256] = dot(
                normed[:, lo : lo + 512], proj[:, a : a + 256], RR
            ).astype(BF)
        out[:, 768:] = dot(branch[:, lo : lo + 512], gated[...], RR).astype(BF)


def body(
    tokens,
    norm_gain,
    in_weight,
    conv_weight,
    out_weight,
    ffn_gain,
    gate_up_weight,
    down_weight,
    cotangent,
):
    in_shape = tokens.shape
    width = in_shape[-1]
    rows = in_shape[1]
    fi = lax.axis_index("fsdp")
    zh, y, core = fi // 8, (fi // 2) % 4, fi % 2
    x = lax.axis_index("tp")
    spots = [x, (x + 3) % 4, (x + 1) % 4, (x + 2) % 4]
    taps = conv_weight.astype(F32)

    ffn_mine = jnp.concatenate([gate_up_weight, down_weight.T[None]], 0)
    ffn_pair = jnp.concatenate([ffn_mine, z_cross(ffn_mine)], 1)
    mine = jnp.concatenate([in_weight.reshape(64, 768), out_weight.T], 1)
    pair = jnp.concatenate([mine, z_cross(mine)], 0)
    col = jnp.concatenate([pair, y_shift(pair, -1), y_shift(pair, 2), y_shift(pair, 1)], 0)
    w_mix = jnp.concatenate([col, core_swap(col)], 0)
    w_in = w_mix[:, :768]
    w_out_t = w_mix[:, 768:]

    above, below = y_shift(ffn_pair, -1), y_shift(ffn_pair, 1)
    spot = jnp.arange(width)
    blk = spot // 64
    source = ((zh ^ (blk % 2)) * 8 + ((y + blk // 2) % 4) * 2 + (core ^ (blk // 8))) * 64 + spot % 64
    order = (jnp.arange(width)[:, None] == source[None, :]).astype(BF)
    tok = dot(tie(tokens.reshape(-1, width), pair), order).astype(BF)
    both_gains = dot(jnp.stack([norm_gain, ffn_gain], 0), order)
    gain1, gain2 = both_gains[0], both_gains[1]

    x32 = tok.astype(F32)
    inv1 = inv_rms_of(x32)
    normed1 = x32 * inv1
    normed_in = (normed1 * gain1).astype(BF)
    projected = dot(normed_in, w_in)
    gate_b, gate_c, values_v = projected[:, :256], projected[:, 256:512], projected[:, 512:]
    mixed_in = (gate_b * values_v).astype(BF)
    arrived = passed_along(mixed_in[rows - 2 :], 1)
    extended = jnp.concatenate([arrived, mixed_in], 0).astype(F32)
    conv_out = (
        taps[0] * extended[:rows] + taps[1] * extended[1 : rows + 1] + taps[2] * extended[2:]
    )
    gated = (gate_c * conv_out).astype(BF)
    gateds = [block(gated, s) for s in spots]
    own_tok = block(tok, x)
    mixer_parts = [dot(g, w_out_t, CC) for g in gateds]
    own_part = tie(own_tok.astype(F32) + mixer_parts[0], above, below)
    middle = summed(own_part, scatter_x(mixer_parts))

    cot = dot(tie(cotangent.reshape(-1, width), *mixer_parts), order).astype(BF)

    above_2, below_2 = tied([above, below], *mixer_parts)
    far = jnp.concatenate([y_shift(above_2[:, :64], -1), y_shift(below_2[:, 64:], 1)], 1)
    inv2 = inv_rms_of(middle)
    normed2 = middle * inv2
    nm = gather_x((normed2 * gain2).astype(BF))
    pair = ffn_pair
    above, below, far = tied([above, below, far], nm[1], nm[2])
    w_ffn = jnp.zeros((3, width, 1152), BF)
    for slot, piece in ((0, pair), (1, above), (3, below), (2, far)):
        w_ffn = lax.dynamic_update_slice_in_dim(w_ffn, piece, slot * 128, 1)
        w_ffn = lax.dynamic_update_slice_in_dim(w_ffn, core_swap(piece), 512 + slot * 128, 1)

    cots = [block(cot, s) for s in spots]
    cot_all = jnp.concatenate(cots, 0)
    nm[3] = tie(nm[3], cot_all)
    piece, hidden = (ROWS, width), (rows, 1152)
    pieces = [(piece, F32), (piece, BF), (piece, BF), (piece, BF)]
    nm_all, gates, ups, act_all, *ffns = local_call(
        ffn_forward,
        [((rows, width), BF), (hidden, F32), (hidden, F32), (hidden, BF), *pieces],
        [*nm, w_ffn],
    )
    got_out = scatter_x(ffns)
    cot_all = tie(cot_all, *ffns)
    half = ((3, 512, 1152), BF)
    g_send, gg_all, gu_all, *mids = local_call(
        ffn_back,
        [half, (hidden, BF), (hidden, BF), *pieces],
        [gates, ups, nm_all, cot_all, act_all, w_ffn],
    )
    out_rows = summed(tie(middle + ffns[0], *mids), got_out)
    got_mid = scatter_x(mids, out_rows)

    g_keep = local_call(
        functools.partial(ffn_grads, 0),
        [half],
        [tie(nm_all, out_rows), cot_all, gg_all, gu_all, act_all],
    )[0]
    h_ffn = add_low(g_keep, core_swap(tie(g_send, out_rows)))
    up_ffn, down_ffn, finish_ffn = reduce_y(h_ffn)
    out_rows = dot(out_rows.astype(BF), order, CC).astype(BF)
    grad_mid_in = summed(tie(mids[0], h_ffn, out_rows), got_mid)

    cot_own = cots[0].astype(F32)
    sv = grad_mid_in * gain2
    grad_middle = cot_own + inv2 * (sv - normed2 * jnp.mean(sv * normed2, -1, keepdims=True))
    gain2_part = jnp.sum(grad_mid_in * normed2, 0)
    mine = grad_middle.astype(BF)
    branches = gather_x(mine)

    grad_gated = place([dot(p, w_out_t) for p in branches], spots)
    grad_c = grad_gated * conv_out
    grad_conv = grad_gated * gate_c
    back = tie(passed_along(grad_conv[:2], -1), up_ffn, down_ffn)
    padded = jnp.concatenate([grad_conv, back], 0)
    grad_mixed = taps[2] * padded[:rows] + taps[1] * padded[1 : rows + 1] + taps[0] * padded[2:]
    rounded = grad_mixed.astype(BF).astype(F32)
    grad_proj = jnp.concatenate([rounded * values_v, grad_c, rounded * gate_b], 1).astype(BF)
    longer = ((ROWS + 16, width), BF)
    own_part, *sent, note = local_call(
        norm_rows,
        [(piece, F32), longer, longer, longer, ((16, width), BF)],
        [jnp.stack(spots).astype(jnp.int32), grad_proj, w_mix, tok, gain2_part[None]],
        first=pltpu.SMEM,
    )
    got_rows = [x_shift(sent[2], 2), x_shift(sent[0], -1), x_shift(sent[1], 1)]

    grad_proj_late, branch_all, grad_conv_late = tied(
        [grad_proj, jnp.concatenate(branches, 0), grad_conv], *sent
    )
    gated_all = jnp.concatenate(gateds, 0)
    taps_part = jnp.stack(
        [
            jnp.sum(extended[:rows] * grad_conv_late, 0),
            jnp.sum(extended[1 : rows + 1] * grad_conv_late, 0),
            jnp.sum(extended[2:] * grad_conv_late, 0),
        ],
        0,
    )

    half = ((512, 1024), BF)
    m_send, m_keep = local_call(
        mix_grads, [half, half], [normed_in, grad_proj_late, branch_all, gated_all]
    )
    m_got = core_swap(m_send)
    taps_row = jnp.concatenate([taps_part[0], taps_part[1], taps_part[2], jnp.zeros((256,), F32)])[None]
    own_part = tie(own_part, m_keep, m_send, taps_row)

    both, small, small_low = local_call(
        last_rows,
        [((2 * ROWS, width), BF), ((8, width), F32), ((16, width), BF)],
        [
            own_part,
            *got_rows,
            note,
            grad_middle,
            own_tok,
            gain1[None],
            order,
            out_rows,
            taps_row,
        ],
    )
    after = paced(small_low, 12, both)
    k_ffn = finish_ffn(after)[0]
    m_keep, m_got = tied([m_keep, m_got], after)
    h_mix = add_low(m_keep, m_got)
    both = gather_x(both)
    both[0] = tie(both[0], both[1])
    input_grad = place([v[:ROWS] for v in both], spots).reshape(in_shape)
    result = place([v[ROWS:] for v in both], spots).reshape(in_shape)

    small = small + joined(core_swap(after))
    up_mix, down_mix, finish_mix = reduce_y(h_mix, split(small))
    k, notes = finish_mix()
    for n in notes:
        small = small + joined(n)
    k = tie(k, both[1], both[2])
    got = z_cross(jnp.concatenate([k[64:].astype(BF), split(small)], 0))
    half = (k[:64] + got[:64].astype(F32)).astype(BF)
    small = small + joined(got[64:])
    got = ctx_swap(jnp.concatenate([half, split(small)], 0))
    r_mix = [half[:, a : a + 256].astype(F32) + got[:64, a : a + 256].astype(F32) for a in (0, 256, 512, 768)]
    small = small + joined(got[64:])
    got = z_cross(k_ffn[:, 64:].astype(BF))
    half_ffn = add_low(k_ffn[:, :64], tie(got, up_mix, down_mix))
    half_ffn = paced(half_ffn, 6, half_ffn)
    got_ffn = ctx_swap(half_ffn)
    return (
        result,
        input_grad,
        small[0],
        jnp.stack(r_mix[:3], 1),
        small[2, :768].reshape(3, 256),
        r_mix[3].T,
        small[1],
        half_ffn[:2].astype(F32) + got_ffn[:2].astype(F32),
        (half_ffn[2].astype(F32) + got_ffn[2].astype(F32)).T,
    )


def solution(mesh):
    placed = (
        P("fsdp", "ctx", None),
        P(),
        P("fsdp", None, "tp"),
        P(None, "tp"),
        P("tp", "fsdp"),
        P(),
        P(None, "fsdp", "tp"),
        P("tp", "fsdp"),
        P("fsdp", "ctx", None),
    )
    return jax.shard_map(
        body,
        mesh=mesh,
        in_specs=placed,
        out_specs=(
            P("fsdp", "ctx", None),
            P("fsdp", "ctx", None),
            P(),
            P("fsdp", None, "tp"),
            P(None, "tp"),
            P("tp", "fsdp"),
            P(),
            P(None, "fsdp", "tp"),
            P("tp", "fsdp"),
        ),
        check_vma=False,
    )
```

```python
import functools

import jax
import jax.numpy as jnp
from jax import lax
from jax.experimental import pallas as pl
from jax.experimental.pallas import tpu as pltpu
from jax.sharding import PartitionSpec as P

EPSILON = 1e-05
BF = jnp.bfloat16
F32 = jnp.float32
NX, NY = 4, 4
ROWS = 192


def x_shift(v, d):
    return lax.ppermute(v, "tp", [(i, (i + d) % NX) for i in range(NX)])


def y_shift(v, d):
    route = []
    for f in range(16):
        zh, y, c = f // 8, (f // 2) % 4, f % 2
        route.append((f, zh * 8 + ((y + d) % NY) * 2 + c))
    return lax.ppermute(v, "fsdp", route)


def core_swap(v):
    return lax.ppermute(v, "fsdp", [(f, f ^ 1) for f in range(16)])


def z_cross(v):
    route = []
    for f in range(16):
        for c in range(2):
            route.append((f * 2 + c, (f ^ 8) * 2 + (c ^ 1)))
    return lax.ppermute(v, ("fsdp", "ctx"), route)


def ctx_swap(v):
    return lax.ppermute(v, "ctx", [(0, 1), (1, 0)])


def passed_along(block, distance):
    route = [(0, 1)] if distance == 1 else [(1, 0)]
    return lax.ppermute(block, "ctx", route)


def dot(a, b, dims=(((1,), (0,)), ((), ()))):
    return lax.dot_general(a, b, dims, preferred_element_type=F32)


CC = (((1,), (1,)), ((), ()))
RR = (((0,), (0,)), ((), ()))


def inv_rms_of(v):
    return lax.rsqrt(jnp.mean(v * v, axis=-1, keepdims=True) + EPSILON)


def place(pieces, spots, axis=0):
    size = pieces[0].shape[axis]
    shape = list(pieces[0].shape)
    shape[axis] = size * len(pieces)
    out = jnp.zeros(shape, pieces[0].dtype)
    for piece, spot in zip(pieces, spots):
        out = lax.dynamic_update_slice_in_dim(out, piece, spot * size, axis)
    return out


def block(v, spot, size=ROWS, axis=0):
    return lax.dynamic_slice_in_dim(v, spot * size, size, axis)


def gather_x(v):
    half = v.shape[0] // 2
    down, up = x_shift(v, 1), x_shift(v, -1)
    far = [x_shift(down[:half], 1), x_shift(up[half:], -1)]
    return [v, down, up, jnp.concatenate(far, 0)]


def tie(v, *deps):
    return lax.optimization_barrier((v,) + deps)[0]


def split(v):
    high = v.astype(BF)
    return jnp.concatenate([high, (v - high.astype(F32)).astype(BF)], 0)


def joined(v):
    half = v.shape[0] // 2
    return v[:half].astype(F32) + v[half:].astype(F32)


def tied(values, *deps):
    return list(lax.optimization_barrier(tuple(values) + deps)[: len(values)])


def scatter_x(parts, *deps):
    one, two, three = tied([p.astype(BF) for p in parts[1:]], *deps)
    return [x_shift(three, 2), x_shift(one, -1), x_shift(two, 1)]


def summed(own, got):
    for part in got:
        own = own + part.astype(F32)
    return own


def add_low(a, b):
    return (a.astype(F32) + b.astype(F32)).astype(BF)


def reduce_y(h, note=None):
    own, up, far, down = (h[..., i : i + 128, :] for i in (0, 128, 256, 384))
    near = far[..., :64, :], far[..., 64:, :]
    if note is not None:
        near = [jnp.concatenate([v, note], 0) for v in near]
    from_below, from_above = y_shift(near[0], 1), y_shift(near[1], -1)
    up = jnp.concatenate([add_low(up[..., :64, :], from_below[..., :64, :]), up[..., 64:, :]], -2)
    down = [down[..., :64, :], add_low(down[..., 64:, :], from_above[..., :64, :])]
    if note is not None:
        down.append(from_above[64:])
    down = jnp.concatenate(down, -2)

    one, two = y_shift(up, 1), y_shift(down, -1)

    def finish(*deps):
        one_, two_ = tied([one, two], *deps)
        k = own.astype(F32) + one_.astype(F32) + two_[..., :128, :].astype(F32)
        notes = [] if note is None else [from_below[64:], from_above[64:], two_[128:]]
        return k, notes

    return up, down, finish


IN_VMEM = pl.BlockSpec(memory_space=pltpu.VMEM)
TILES = [(a, min(a + 256, 1152)) for a in range(0, 1152, 256)]


def local_call(kernel, outs, args, first=pltpu.VMEM):
    return pl.pallas_call(
        kernel,
        out_shape=[jax.ShapeDtypeStruct(shape, dtype) for shape, dtype in outs],
        in_specs=[pl.BlockSpec(memory_space=first)] + [IN_VMEM] * (len(args) - 1),
        out_specs=[IN_VMEM] * len(outs),
        compiler_params=pltpu.CompilerParams(vmem_limit_bytes=8 * 2**20),
        cost_estimate=pl.CostEstimate(flops=1024, bytes_accessed=1024, transcendentals=0),
    )(*args)


def mark(v, *refs):
    refs[-1][...] = v[...]


def paced(v, us, *deps):
    return pl.pallas_call(
        mark,
        out_shape=jax.ShapeDtypeStruct(v.shape, v.dtype),
        in_specs=[IN_VMEM] + [pl.BlockSpec(memory_space=pl.ANY)] * len(deps),
        out_specs=IN_VMEM,
        compiler_params=pltpu.CompilerParams(vmem_limit_bytes=2**20),
        cost_estimate=pl.CostEstimate(
            flops=us * 10**9, bytes_accessed=us * 3 * 10**6, transcendentals=0
        ),
    )(v, *deps)


def ffn_forward(*refs):
    pieces, w = refs[:4], refs[4]
    nm, gate, up, act = refs[5:9]
    outs = refs[9:13]
    for i in range(4):
        nm[i * ROWS : (i + 1) * ROWS, :] = pieces[i][...]
    for a, b in TILES:
        gate_g = dot(nm[...], w[0, :, a:b])
        up_u = dot(nm[...], w[1, :, a:b])
        gate[:, a:b] = gate_g
        up[:, a:b] = up_u
        act[:, a:b] = (gate_g * (1.0 / (1.0 + jnp.exp(-gate_g))) * up_u).astype(BF)
    for a in range(0, 1024, 256):
        part = dot(act[...], w[2, a : a + 256, :], CC)
        for i in range(4):
            outs[i][:, a : a + 256] = part[i * ROWS : (i + 1) * ROWS].astype(outs[i].dtype)


def ffn_back(gate, up, nm, cot, act, w, send, gg, gu, *mids):
    for a, b in TILES:
        grad_act = dot(cot[...], w[2, :, a:b])
        gate_g = gate[:, a:b]
        sg = 1.0 / (1.0 + jnp.exp(-gate_g))
        gg[:, a:b] = (grad_act * up[:, a:b] * sg * (1.0 + gate_g * (1.0 - sg))).astype(BF)
        gu[:, a:b] = (grad_act * (gate_g * sg)).astype(BF)
    for a in range(0, 1024, 256):
        part = dot(gg[...], w[0, a : a + 256, :], CC) + dot(gu[...], w[1, a : a + 256, :], CC)
        for i in range(4):
            mids[i][:, a : a + 256] = part[i * ROWS : (i + 1) * ROWS].astype(mids[i].dtype)
    ffn_grads(512, nm, cot, gg, gu, act, send)


def ffn_grads(lo, nm, cot, gg, gu, act, out):
    for k, left, right in ((0, nm, gg), (1, nm, gu), (2, cot, act)):
        for a, b in TILES:
            out[k, :, a:b] = dot(left[:, lo : lo + 512], right[:, a:b], RR).astype(BF)


def norm_rows(spots, proj, w_mix, tok, gain2, own, one, two, three, note):
    gain1 = jnp.zeros((1, 1024), F32)
    for i, out in ((3, three), (1, one), (2, two), (0, own)):
        span = pl.ds(pl.multiple_of(spots[i] * ROWS, ROWS), ROWS)
        part = dot(proj[span, :], w_mix[:, :768], CC)
        x32 = tok[span, :].astype(F32)
        inv = lax.rsqrt(jnp.mean(x32 * x32, axis=-1, keepdims=True) + EPSILON)
        gain1 += jnp.sum(part * (x32 * inv), axis=0, keepdims=True)
        out[:ROWS, :] = part.astype(out.dtype)
    at = lax.broadcasted_iota(jnp.int32, (16, 1024), 0)
    note[...] = jnp.zeros((16, 1024), BF)
    for k, v in ((0, gain1), (1, gain2[...])):
        high = v.astype(BF).astype(F32)
        now = jnp.where(at == k, high, jnp.where(at == k + 2, v - high, note[...].astype(F32)))
        note[...] = now.astype(BF)
    for out in (one, two, three):
        out[ROWS:, :] = note[...]


def last_rows(own, one, two, three, note, grad_middle, tok, gain, order, done, taps, out, small, low):
    total = own[...]
    notes = note[...].astype(F32)
    for got in (one, two, three):
        total += got[:ROWS].astype(F32)
        notes += got[ROWS:].astype(F32)
    x32 = tok[...].astype(F32)
    inv = lax.rsqrt(jnp.mean(x32 * x32, axis=-1, keepdims=True) + EPSILON)
    normed = x32 * inv
    su = total * gain[...]
    rows = grad_middle[...] + inv * (su - normed * jnp.mean(su * normed, -1, keepdims=True))
    out[:ROWS, :] = dot(rows.astype(BF), order[...], CC).astype(BF)
    out[ROWS:, :] = done[...]
    at = lax.broadcasted_iota(jnp.int32, (8, 1024), 0)
    both = notes[0:2] + notes[2:4]
    high = both.astype(BF)
    rest = (both - high.astype(F32)).astype(BF)
    true = dot(high, order[...], CC) + dot(rest, order[...], CC)
    now = jnp.where(at == 0, true[0:1], jnp.where(at == 1, true[1:2], jnp.where(at == 2, taps[...], 0.0)))
    small[...] = now
    low[0:8, :] = now.astype(BF)
    low[8:16, :] = (now - now.astype(BF).astype(F32)).astype(BF)


def mix_grads(normed, proj, branch, gated, send, keep):
    for out, lo in ((send, 512), (keep, 0)):
        for a in range(0, 768, 256):
            out[:, a : a + 256] = dot(
                normed[:, lo : lo + 512], proj[:, a : a + 256], RR
            ).astype(BF)
        out[:, 768:] = dot(branch[:, lo : lo + 512], gated[...], RR).astype(BF)


def body(
    tokens,
    norm_gain,
    in_weight,
    conv_weight,
    out_weight,
    ffn_gain,
    gate_up_weight,
    down_weight,
    cotangent,
):
    in_shape = tokens.shape
    width = in_shape[-1]
    rows = in_shape[1]
    fi = lax.axis_index("fsdp")
    zh, y, core = fi // 8, (fi // 2) % 4, fi % 2
    x = lax.axis_index("tp")
    spots = [x, (x + 3) % 4, (x + 1) % 4, (x + 2) % 4]
    taps = conv_weight.astype(F32)

    ffn_mine = jnp.concatenate([gate_up_weight, down_weight.T[None]], 0)
    ffn_pair = jnp.concatenate([ffn_mine, z_cross(ffn_mine)], 1)
    mine = jnp.concatenate([in_weight.reshape(64, 768), out_weight.T], 1)
    pair = jnp.concatenate([mine, z_cross(mine)], 0)
    col = jnp.concatenate([pair, y_shift(pair, -1), y_shift(pair, 2), y_shift(pair, 1)], 0)
    w_mix = jnp.concatenate([col, core_swap(col)], 0)
    w_in = w_mix[:, :768]
    w_out_t = w_mix[:, 768:]

    above, below = y_shift(ffn_pair, -1), y_shift(ffn_pair, 1)
    spot = jnp.arange(width)
    blk = spot // 64
    source = ((zh ^ (blk % 2)) * 8 + ((y + blk // 2) % 4) * 2 + (core ^ (blk // 8))) * 64 + spot % 64
    order = (jnp.arange(width)[:, None] == source[None, :]).astype(BF)
    tok = dot(tie(tokens.reshape(-1, width), pair), order).astype(BF)
    both_gains = dot(jnp.stack([norm_gain, ffn_gain], 0), order)
    gain1, gain2 = both_gains[0], both_gains[1]

    x32 = tok.astype(F32)
    inv1 = inv_rms_of(x32)
    normed1 = x32 * inv1
    normed_in = (normed1 * gain1).astype(BF)
    projected = dot(normed_in, w_in)
    gate_b, gate_c, values_v = projected[:, :256], projected[:, 256:512], projected[:, 512:]
    mixed_in = (gate_b * values_v).astype(BF)
    arrived = passed_along(mixed_in[rows - 2 :], 1)
    extended = jnp.concatenate([arrived, mixed_in], 0).astype(F32)
    conv_out = (
        taps[0] * extended[:rows] + taps[1] * extended[1 : rows + 1] + taps[2] * extended[2:]
    )
    gated = (gate_c * conv_out).astype(BF)
    gateds = [block(gated, s) for s in spots]
    own_tok = block(tok, x)
    mixer_parts = [dot(g, w_out_t, CC) for g in gateds]
    own_part = tie(own_tok.astype(F32) + mixer_parts[0], above, below)
    middle = summed(own_part, scatter_x(mixer_parts))

    cot = dot(tie(cotangent.reshape(-1, width), *mixer_parts), order).astype(BF)

    above_2, below_2 = tied([above, below], *mixer_parts)
    far = jnp.concatenate([y_shift(above_2[:, :64], -1), y_shift(below_2[:, 64:], 1)], 1)
    inv2 = inv_rms_of(middle)
    normed2 = middle * inv2
    nm = gather_x((normed2 * gain2).astype(BF))
    pair = ffn_pair
    above, below, far = tied([above, below, far], nm[1], nm[2])
    w_ffn = jnp.zeros((3, width, 1152), BF)
    for slot, piece in ((0, pair), (1, above), (3, below), (2, far)):
        w_ffn = lax.dynamic_update_slice_in_dim(w_ffn, piece, slot * 128, 1)
        w_ffn = lax.dynamic_update_slice_in_dim(w_ffn, core_swap(piece), 512 + slot * 128, 1)

    cots = [block(cot, s) for s in spots]
    cot_all = jnp.concatenate(cots, 0)
    nm[3] = tie(nm[3], cot_all)
    piece, hidden = (ROWS, width), (rows, 1152)
    pieces = [(piece, F32), (piece, BF), (piece, BF), (piece, BF)]
    nm_all, gates, ups, act_all, *ffns = local_call(
        ffn_forward,
        [((rows, width), BF), (hidden, F32), (hidden, F32), (hidden, BF), *pieces],
        [*nm, w_ffn],
    )
    got_out = scatter_x(ffns)
    cot_all = tie(cot_all, *ffns)
    half = ((3, 512, 1152), BF)
    g_send, gg_all, gu_all, *mids = local_call(
        ffn_back,
        [half, (hidden, BF), (hidden, BF), *pieces],
        [gates, ups, nm_all, cot_all, act_all, w_ffn],
    )
    out_rows = summed(tie(middle + ffns[0], *mids), got_out)
    got_mid = scatter_x(mids, out_rows)

    g_keep = local_call(
        functools.partial(ffn_grads, 0),
        [half],
        [tie(nm_all, out_rows), cot_all, gg_all, gu_all, act_all],
    )[0]
    h_ffn = add_low(g_keep, core_swap(tie(g_send, out_rows)))
    up_ffn, down_ffn, finish_ffn = reduce_y(h_ffn)
    out_rows = dot(out_rows.astype(BF), order, CC).astype(BF)
    grad_mid_in = summed(tie(mids[0], h_ffn, out_rows), got_mid)

    cot_own = cots[0].astype(F32)
    sv = grad_mid_in * gain2
    grad_middle = cot_own + inv2 * (sv - normed2 * jnp.mean(sv * normed2, -1, keepdims=True))
    gain2_part = jnp.sum(grad_mid_in * normed2, 0)
    mine = grad_middle.astype(BF)
    branches = gather_x(mine)

    grad_gated = place([dot(p, w_out_t) for p in branches], spots)
    grad_c = grad_gated * conv_out
    grad_conv = grad_gated * gate_c
    back = tie(passed_along(grad_conv[:2], -1), up_ffn, down_ffn)
    padded = jnp.concatenate([grad_conv, back], 0)
    grad_mixed = taps[2] * padded[:rows] + taps[1] * padded[1 : rows + 1] + taps[0] * padded[2:]
    rounded = grad_mixed.astype(BF).astype(F32)
    grad_proj = jnp.concatenate([rounded * values_v, grad_c, rounded * gate_b], 1).astype(BF)
    longer = ((ROWS + 16, width), BF)
    own_part, *sent, note = local_call(
        norm_rows,
        [(piece, F32), longer, longer, longer, ((16, width), BF)],
        [jnp.stack(spots).astype(jnp.int32), grad_proj, w_mix, tok, gain2_part[None]],
        first=pltpu.SMEM,
    )
    got_rows = [x_shift(sent[2], 2), x_shift(sent[0], -1), x_shift(sent[1], 1)]

    grad_proj_late, branch_all, grad_conv_late = tied(
        [grad_proj, jnp.concatenate(branches, 0), grad_conv], *sent
    )
    gated_all = jnp.concatenate(gateds, 0)
    taps_part = jnp.stack(
        [
            jnp.sum(extended[:rows] * grad_conv_late, 0),
            jnp.sum(extended[1 : rows + 1] * grad_conv_late, 0),
            jnp.sum(extended[2:] * grad_conv_late, 0),
        ],
        0,
    )

    half = ((512, 1024), BF)
    m_send, m_keep = local_call(
        mix_grads, [half, half], [normed_in, grad_proj_late, branch_all, gated_all]
    )
    m_got = core_swap(m_send)
    taps_row = jnp.concatenate([taps_part[0], taps_part[1], taps_part[2], jnp.zeros((256,), F32)])[None]
    own_part = tie(own_part, m_keep, m_send, taps_row)

    both, small, small_low = local_call(
        last_rows,
        [((2 * ROWS, width), BF), ((8, width), F32), ((16, width), BF)],
        [
            own_part,
            *got_rows,
            note,
            grad_middle,
            own_tok,
            gain1[None],
            order,
            out_rows,
            taps_row,
        ],
    )
    after = paced(small_low, 25, both)
    k_ffn = finish_ffn(after)[0]
    m_keep, m_got = tied([m_keep, m_got], after)
    h_mix = add_low(m_keep, m_got)
    both = gather_x(both)
    both[0] = tie(both[0], both[1])
    input_grad = place([v[:ROWS] for v in both], spots).reshape(in_shape)
    result = place([v[ROWS:] for v in both], spots).reshape(in_shape)

    small = small + joined(core_swap(after))
    up_mix, down_mix, finish_mix = reduce_y(h_mix, split(small))
    k, notes = finish_mix()
    for n in notes:
        small = small + joined(n)
    k = tie(k, both[1], both[2])
    got = z_cross(jnp.concatenate([k[64:].astype(BF), split(small)], 0))
    half = (k[:64] + got[:64].astype(F32)).astype(BF)
    small = small + joined(got[64:])
    got = ctx_swap(jnp.concatenate([half, split(small)], 0))
    r_mix = [half[:, a : a + 256].astype(F32) + got[:64, a : a + 256].astype(F32) for a in (0, 256, 512, 768)]
    small = small + joined(got[64:])
    got = z_cross(k_ffn[:, 64:].astype(BF))
    half_ffn = add_low(k_ffn[:, :64], tie(got, up_mix, down_mix))
    half_ffn = paced(half_ffn, 6, half_ffn)
    got_ffn = ctx_swap(half_ffn)
    return (
        result,
        input_grad,
        small[0],
        jnp.stack(r_mix[:3], 1),
        small[2, :768].reshape(3, 256),
        r_mix[3].T,
        small[1],
        half_ffn[:2].astype(F32) + got_ffn[:2].astype(F32),
        (half_ffn[2].astype(F32) + got_ffn[2].astype(F32)).T,
    )


def solution(mesh):
    placed = (
        P("fsdp", "ctx", None),
        P(),
        P("fsdp", None, "tp"),
        P(None, "tp"),
        P("tp", "fsdp"),
        P(),
        P(None, "fsdp", "tp"),
        P("tp", "fsdp"),
        P("fsdp", "ctx", None),
    )
    return jax.shard_map(
        body,
        mesh=mesh,
        in_specs=placed,
        out_specs=(
            P("fsdp", "ctx", None),
            P("fsdp", "ctx", None),
            P(),
            P("fsdp", None, "tp"),
            P(None, "tp"),
            P("tp", "fsdp"),
            P(),
            P(None, "fsdp", "tp"),
            P("tp", "fsdp"),
        ),
        check_vma=False,
    )
```
